512 devices in a mesh: outer: 32 (over z, y_lo), inner: 16 (over y_hi, x, core).
Axes of the slice: x: 4, y: 8 (y_hi: 2, y_lo: 4; y = y_hi * 4 + y_lo), z: 8, core: 2. Of those that a mesh axis runs over, the one named last changes fastest.
Arguments:
- queries: bfloat16 [65536, 1280], P(('outer', 'inner')), may hold values from -1.5 to 1.5
- key_states: bfloat16 [65536, 1280], P(('outer', 'inner')), may hold values from -3 to 3
- value_states: bfloat16 [65536, 1280], P(('outer', 'inner')), may hold values from -4 to 4
- out_grad: bfloat16 [65536, 1280], P(('outer', 'inner')), may hold values from -96 to 96
- log_total: float32 [20, 65536], P(None, ('outer', 'inner')), may hold values from 5 to 8.5
- row_delta: float32 [20, 65536], P(None, ('outer', 'inner')), may hold values from -256 to 256
Outputs:
- query_grad: bfloat16 [65536, 1280], P(('outer', 'inner'))
- key_grad: bfloat16 [65536, 1280], P(('outer', 'inner'))
- value_grad: bfloat16 [65536, 1280], P(('outer', 'inner'))
The draws below stay inside these ranges and needn't reach their ends.
All inputs are finite; a program needn't handle non-finite values.
Results may differ from the reference program's by a relative error of at most 0.0049.
Values may be sent and summed in bfloat16 or wider, within the bound.
A program may use at most 64 MiB of HBM per device.

```python
import jax
import jax.numpy as jnp
from jax import lax

HEADS = 20
HEAD_DIM = 64
TOK_DEV = 128
OUTER_STEPS = 2
INNER_PASSES = 2
WIDTH = 1280
TOKENS = 65536
N_OUTER = 32
N_INNER = 16


def block_levels(own_key, shape, pieces, low, top_value):
    loudness, own = 1.0, jax.random.fold_in(own_key, 6)
    for axis_at, parts in pieces:
        draws = jnp.exp(jax.random.uniform(jax.random.fold_in(own, axis_at), (parts,), jnp.float32, low / len(pieces), top_value / len(pieces)))
        loudness = loudness * jnp.repeat(draws, shape[axis_at] // parts).reshape([-1 if axis == axis_at else 1 for axis in range(len(shape))])
    return loudness


def gaussian(stream_key, shape, width, limit, pieces=(), held_as=jnp.bfloat16):
    values = jax.random.normal(stream_key, shape, jnp.float32) * width
    if len(pieces) > 0:
        values = block_levels(stream_key, shape, pieces, -0.22, 0.18) * values
    return jnp.clip(values, min=-limit, max=limit).astype(held_as)


def setup_inputs(seed: int = 0) -> dict:
    arg_keys = jax.random.split(jax.random.key(seed), 7)
    queries = gaussian(arg_keys[0], (TOKENS, WIDTH), 0.5, 1.5, ((0, 512),))
    key_states = gaussian(arg_keys[1], (TOKENS, WIDTH), 1.0, 3.0, ((0, 512),))
    value_states = gaussian(arg_keys[2], (TOKENS, WIDTH), 1.0, 4.0, ((0, 512),))
    out_grad = gaussian(arg_keys[3], (TOKENS, WIDTH), 16.0, 96.0, ((0, 512),))
    log_total = jnp.clip(5.0 + 3.5 * jax.random.uniform(arg_keys[4], (HEADS, TOKENS), jnp.float32) ** block_levels(arg_keys[4], (HEADS, TOKENS), ((1, 512),), -0.2, 0.2), 5.0, 8.5)
    row_delta = gaussian(arg_keys[5], (HEADS, TOKENS), 64.0, 256.0, ((1, 512),), jnp.float32)
    return dict(queries=queries, key_states=key_states, value_states=value_states, out_grad=out_grad, log_total=log_total, row_delta=row_delta)


def block_terms(items):
    queries, grads_out, log_local, delta_local, key_block, value_block = items
    scale = HEAD_DIM ** -0.5
    query_f = queries.astype(jnp.float32)
    grad_f = grads_out.astype(jnp.float32)
    key_f = key_block.astype(jnp.float32)
    value_f = value_block.astype(jnp.float32)
    scores = jnp.einsum("qhd,khd->hqk", query_f, key_f) * scale
    probs = jnp.exp(scores - log_local[:, :, None])
    probs_low = probs.astype(jnp.bfloat16).astype(jnp.float32)
    dprobs = jnp.einsum("qhd,khd->hqk", grad_f, value_f)
    score_grad = (probs * (dprobs - delta_local[:, :, None])).astype(jnp.bfloat16).astype(jnp.float32)
    query_part = jnp.einsum("hqk,khd->qhd", score_grad, key_f)
    key_part = jnp.einsum("hqk,qhd->khd", score_grad, query_f)
    value_part = jnp.einsum("hqk,qhd->khd", probs_low, grad_f)
    return query_part, key_part, value_part


def reference(queries, key_states, value_states, out_grad, log_total, row_delta):
    blocks = N_OUTER * N_INNER
    grid_shape = (N_OUTER, N_INNER, TOK_DEV, WIDTH)
    split_shape = (blocks, TOK_DEV, HEADS, HEAD_DIM)
    query_blocks = queries.reshape(split_shape)
    grad_blocks = out_grad.reshape(split_shape)
    log_blocks = log_total.reshape(HEADS, blocks, TOK_DEV).transpose(1, 0, 2)
    delta_blocks = row_delta.reshape(HEADS, blocks, TOK_DEV).transpose(1, 0, 2)
    key_grid = key_states.reshape(grid_shape)
    value_grid = value_states.reshape(grid_shape)
    query_sum = jnp.zeros(grid_shape, jnp.float32)
    key_sum = jnp.zeros(grid_shape, jnp.float32)
    value_sum = jnp.zeros(grid_shape, jnp.float32)
    for outer_step in range(OUTER_STEPS):
        for inner_pass in range(INNER_PASSES):
            key_pair = jnp.roll(key_grid, (outer_step, inner_pass), axis=(0, 1)).reshape(split_shape)
            value_pair = jnp.roll(value_grid, (outer_step, inner_pass), axis=(0, 1)).reshape(split_shape)
            query_part, key_part, value_part = lax.map(block_terms, (query_blocks, grad_blocks, log_blocks, delta_blocks, key_pair, value_pair))
            query_sum = query_sum + query_part.reshape(grid_shape)
            key_sum = key_sum + jnp.roll(key_part.reshape(grid_shape), (-outer_step, -inner_pass), axis=(0, 1))
            value_sum = value_sum + jnp.roll(value_part.reshape(grid_shape), (-outer_step, -inner_pass), axis=(0, 1))
    scale = HEAD_DIM ** -0.5
    query_grad = (query_sum * scale).reshape(TOKENS, WIDTH).astype(jnp.bfloat16)
    key_grad = (key_sum * scale).reshape(TOKENS, WIDTH).astype(jnp.bfloat16)
    value_grad = value_sum.reshape(TOKENS, WIDTH).astype(jnp.bfloat16)
    return query_grad, key_grad, value_grad
```

```python
import functools
import math

import jax
import jax.numpy as jnp
from jax import lax
from jax.experimental import pallas as pl
from jax.experimental.pallas import tpu as pltpu
from jax.sharding import PartitionSpec as P

HEAD_DIM = 64
SCALE = HEAD_DIM ** (-0.5)
LOG2E = math.log2(math.e)
LANES = 128
MESH = pl.DeviceIdType.MESH
NT = (((1,), (1,)), ((), ()))
NN = (((1,), (0,)), ((), ()))
TN = (((0,), (0,)), ((), ()))


def mm(a, b, dims):
    return lax.dot_general(a, b, dims, preferred_element_type=jnp.float32)


def kernel(
    n_outer, n_inner, chunks,
    q_hbm, k_hbm, v_hbm, g_hbm, log_hbm, delta_hbm,
    dq_hbm, dk_hbm, dv_hbm,
    qg, kv, stats, dq_own, dkv_own, dq_send, dkv_send, dq_recv, dkv_recv, out,
    stage_sem, stat_sem, qg_send_sem, qg_recv_sem, kv_send_sem, kv_recv_sem,
    st_send_sem, st_recv_sem, dq_send_sem, dq_recv_sem, dkv_send_sem, dkv_recv_sem, out_sem,
):
    o, i = lax.axis_index("outer"), lax.axis_index("inner")
    up = (lax.rem(o + 1, n_outer), i)
    down = (lax.rem(o + n_outer - 1, n_outer), i)
    right = (o, lax.rem(i + 1, n_inner))
    left = (o, lax.rem(i + n_inner - 1, n_inner))

    def columns(c):
        return pl.ds(pl.multiple_of(c * LANES, LANES), LANES)

    def stage(c):
        sources = ((q_hbm, qg, 0), (g_hbm, qg, 1), (k_hbm, kv, 0), (v_hbm, kv, 1))
        return [
            pltpu.make_async_copy(src.at[:, columns(c)], dst.at[c, 0, at], stage_sem.at[c, n])
            for n, (src, dst, at) in enumerate(sources)
        ]

    def remote(src, dst, send, recv, device):
        return pltpu.make_async_remote_copy(
            src_ref=src, dst_ref=dst, send_sem=send, recv_sem=recv,
            device_id=device, device_id_type=MESH,
        )

    def send_qg(c):
        return remote(qg.at[c, 0], qg.at[c, 1], qg_send_sem.at[c], qg_recv_sem.at[c], down)

    def send_kv(c):
        return remote(kv.at[c, 0], kv.at[c, 1], kv_send_sem.at[c], kv_recv_sem.at[c], right)

    def send_stats(n):
        return remote(stats.at[0, n], stats.at[1, n], st_send_sem.at[n], st_recv_sem.at[n], down)

    def send_dq(c):
        return remote(dq_send.at[c], dq_recv.at[c], dq_send_sem.at[c], dq_recv_sem.at[c], up)

    def send_dkv(c):
        return remote(dkv_send.at[c], dkv_recv.at[c], dkv_send_sem.at[c], dkv_recv_sem.at[c], left)

    def write(c):
        return [
            pltpu.make_async_copy(out.at[n, c], dst.at[:, columns(c)], out_sem.at[c, n])
            for n, dst in enumerate((dq_hbm, dk_hbm, dv_hbm))
        ]

    stat_copies = [
        pltpu.make_async_copy(src, stats.at[0, n], stat_sem.at[n])
        for n, src in enumerate((log_hbm, delta_hbm))
    ]
    for copy in stat_copies:
        copy.start()

    @pl.loop(0, chunks)
    def _(c):
        for copy in stage(c):
            copy.start()

    barrier = pltpu.get_barrier_semaphore()
    for device in (up, down, right, left):
        pl.semaphore_signal(barrier, inc=1, device_id=device, device_id_type=MESH)
    pl.semaphore_wait(barrier, 4)

    for n, copy in enumerate(stat_copies):
        copy.wait()
        send_stats(n).start()

    @pl.loop(0, chunks)
    def _(c):
        for copy in stage(c):
            copy.wait()
        send_qg(c).start()
        send_kv(c).start()

    for n in range(2):
        send_stats(n).wait_recv()

    first_head = lax.broadcasted_iota(jnp.int32, (1, LANES), 1) < HEAD_DIM

    @pl.loop(0, chunks)
    def _(c):
        send_qg(c).wait_recv()
        send_kv(c).wait_recv()
        queries = jnp.concatenate([qg[c, 0, 0], qg[c, 1, 0]], axis=0)
        grads = jnp.concatenate([qg[c, 0, 1], qg[c, 1, 1]], axis=0)
        keys = jnp.concatenate([kv[c, 0, 0], kv[c, 1, 0]], axis=0)
        values = jnp.concatenate([kv[c, 0, 1], kv[c, 1, 1]], axis=0)
        dq = None
        dks, dvs = [], []
        for head in range(2):
            mine = first_head if head == 0 else jnp.logical_not(first_head)
            row = 2 * c + head
            logs = jnp.concatenate([stats[0, 0, pl.ds(row, 1), :], stats[1, 0, pl.ds(row, 1), :]], axis=1)
            deltas = jnp.concatenate([stats[0, 1, pl.ds(row, 1), :], stats[1, 1, pl.ds(row, 1), :]], axis=1)
            keys_h = jnp.where(mine, keys, jnp.zeros_like(keys))
            values_h = jnp.where(mine, values, jnp.zeros_like(values))
            scores = mm(keys_h, queries, NT)
            probs = jnp.exp2(scores * (SCALE * LOG2E) - logs * LOG2E)
            dprobs = mm(values_h, grads, NT)
            score_grad = (probs * (dprobs - deltas)).astype(jnp.bfloat16)
            dvs.append(mm(probs.astype(jnp.bfloat16), grads, NN))
            dks.append(mm(score_grad, queries, NN))
            part = mm(score_grad, keys_h, TN)
            dq = part if dq is None else dq + part
        dk = jnp.where(first_head, dks[0], dks[1]) * SCALE
        dv = jnp.where(first_head, dvs[0], dvs[1])
        dq = dq * SCALE
        rows = dq.shape[0] // 2
        dq_send[c] = dq[rows:].astype(jnp.bfloat16)
        send_dq(c).start()
        dkv_send[c, 0] = dk[rows:].astype(jnp.bfloat16)
        dkv_send[c, 1] = dv[rows:].astype(jnp.bfloat16)
        send_dkv(c).start()
        dq_own[c] = dq[:rows]
        dkv_own[c, 0] = dk[:rows]
        dkv_own[c, 1] = dv[:rows]

    @pl.loop(0, chunks)
    def _(c):
        send_dq(c).wait_recv()
        out[0, c] = (dq_own[c] + dq_recv[c].astype(jnp.float32)).astype(jnp.bfloat16)
        send_dkv(c).wait_recv()
        for n in range(2):
            total = dkv_own[c, n] + dkv_recv[c, n].astype(jnp.float32)
            out[1 + n, c] = total.astype(jnp.bfloat16)
        for copy in write(c):
            copy.start()

    for n in range(2):
        send_stats(n).wait_send()

    @pl.loop(0, chunks)
    def _(c):
        send_qg(c).wait_send()
        send_kv(c).wait_send()
        send_dq(c).wait_send()
        send_dkv(c).wait_send()
        for copy in write(c):
            copy.wait()


def body(queries, key_states, value_states, out_grad, log_total, row_delta):
    rows, width = queries.shape
    heads = log_total.shape[0]
    chunks = width // LANES
    dma = pltpu.SemaphoreType.DMA
    low, full = jnp.bfloat16, jnp.float32
    block = jax.ShapeDtypeStruct((rows, width), low)
    return pl.pallas_call(
        functools.partial(
            kernel, lax.axis_size("outer"), lax.axis_size("inner"), chunks
        ),
        out_shape=(block, block, block),
        in_specs=[pl.BlockSpec(memory_space=pl.ANY)] * 6,
        out_specs=[pl.BlockSpec(memory_space=pl.ANY)] * 3,
        scratch_shapes=[
            pltpu.VMEM((chunks, 2, 2, rows, LANES), low),
            pltpu.VMEM((chunks, 2, 2, rows, LANES), low),
            pltpu.VMEM((2, 2, heads, rows), full),
            pltpu.VMEM((chunks, rows, LANES), full),
            pltpu.VMEM((chunks, 2, rows, LANES), full),
            pltpu.VMEM((chunks, rows, LANES), low),
            pltpu.VMEM((chunks, 2, rows, LANES), low),
            pltpu.VMEM((chunks, rows, LANES), low),
            pltpu.VMEM((chunks, 2, rows, LANES), low),
            pltpu.VMEM((3, chunks, rows, LANES), low),
            dma((chunks, 4)), dma((2,)),
            dma((chunks,)), dma((chunks,)), dma((chunks,)), dma((chunks,)),
            dma((2,)), dma((2,)),
            dma((chunks,)), dma((chunks,)), dma((chunks,)), dma((chunks,)),
            dma((chunks, 3)),
        ],
        compiler_params=pltpu.CompilerParams(
            collective_id=0, has_side_effects=True, vmem_limit_bytes=40 * 2**20
        ),
        cost_estimate=pl.CostEstimate(
            flops=40 * rows * rows * width, bytes_accessed=14 * rows * width,
            transcendentals=4 * heads * rows * rows,
        ),
        name="window_backward",
    )(queries, key_states, value_states, out_grad, log_total, row_delta)


def solution(mesh):
    tokens = P(("outer", "inner"), None)
    stats = P(None, ("outer", "inner"))
    return jax.shard_map(
        body,
        mesh=mesh,
        in_specs=(tokens, tokens, tokens, tokens, stats, stats),
        out_specs=(tokens, tokens, tokens),
        check_vma=False,
    )
```

```python
import functools
import math

import jax
import jax.numpy as jnp
from jax import lax
from jax.experimental import pallas as pl
from jax.experimental.pallas import tpu as pltpu
from jax.sharding import PartitionSpec as P

HEAD_DIM = 64
SCALE = HEAD_DIM ** (-0.5)
LOG2E = math.log2(math.e)
LANES = 128
RUN = 8
MESH = pl.DeviceIdType.MESH
NT = (((1,), (1,)), ((), ()))
NN = (((1,), (0,)), ((), ()))
TN = (((0,), (0,)), ((), ()))


def mm(a, b, dims):
    return lax.dot_general(a, b, dims, preferred_element_type=jnp.float32)


def kernel(
    n_outer, n_inner, chunks,
    q_hbm, k_hbm, v_hbm, g_hbm, log_hbm, delta_hbm,
    dq_hbm, dk_hbm, dv_hbm,
    qg, kv, relay, stats, dq_own, dkv_own, dq_send, dkv_send, dq_recv, dkv_recv, out,
    stage_sem, stat_sem, qg_send_sem, qg_recv_sem, kv_send_sem, kv_recv_sem,
    st_send_sem, st_recv_sem, dq_send_sem, dq_recv_sem, dkv_send_sem, dkv_recv_sem, out_sem,
    relay_send_sem, relay_recv_sem,
):
    o, i = lax.axis_index("outer"), lax.axis_index("inner")
    up = (lax.rem(o + 1, n_outer), i)
    down = (lax.rem(o + n_outer - 1, n_outer), i)
    right = (o, lax.rem(i + 1, n_inner))
    left = (o, lax.rem(i + n_inner - 1, n_inner))

    place = lax.rem(i, RUN)
    sends_keys, sends_sums = place == RUN - 1, place == 0
    relays_keys, relays_sums = place == RUN - 3, place == 2
    relays = jnp.logical_or(relays_keys, relays_sums)
    ends = jnp.logical_or(sends_keys, sends_sums)

    def along(distance):
        return (o, lax.rem(i + (distance + n_inner), n_inner))

    partners = (
        (sends_keys, (-2, 3)), (sends_sums, (-3, 2)), (relays_keys, (2, 3)), (relays_sums, (-2, -3)),
    )

    def columns(c):
        return pl.ds(pl.multiple_of(c * LANES, LANES), LANES)

    def stage(c):
        sources = ((q_hbm, qg, 0), (g_hbm, qg, 1), (k_hbm, kv, 0), (v_hbm, kv, 1))
        return [
            pltpu.make_async_copy(src.at[:, columns(c)], dst.at[c, 0, at], stage_sem.at[c, n])
            for n, (src, dst, at) in enumerate(sources)
        ]

    def remote(src, dst, send, recv, device):
        return pltpu.make_async_remote_copy(
            src_ref=src, dst_ref=dst, send_sem=send, recv_sem=recv,
            device_id=device, device_id_type=MESH,
        )

    def send_qg(c):
        return remote(qg.at[c, 0], qg.at[c, 1], qg_send_sem.at[c], qg_recv_sem.at[c], down)

    def send_kv(c):
        return remote(kv.at[c, 0], kv.at[c, 1], kv_send_sem.at[c], kv_recv_sem.at[c], right)

    def send_kv_relay(c):
        return remote(kv.at[c, 0], relay.at[c // 2], kv_send_sem.at[c], relay_recv_sem.at[c // 2], along(-2))

    def pass_kv(c):
        return remote(
            relay.at[c // 2], kv.at[c, 1], relay_send_sem.at[c // 2], kv_recv_sem.at[c], along(3)
        )

    def send_stats(n):
        return remote(stats.at[0, n], stats.at[1, n], st_send_sem.at[n], st_recv_sem.at[n], down)

    def send_dq(c):
        return remote(dq_send.at[c], dq_recv.at[c], dq_send_sem.at[c], dq_recv_sem.at[c], up)

    def send_dkv(c):
        return remote(dkv_send.at[c], dkv_recv.at[c], dkv_send_sem.at[c], dkv_recv_sem.at[c], left)

    def send_dkv_relay(c):
        return remote(
            dkv_send.at[c], relay.at[c // 2], dkv_send_sem.at[c], relay_recv_sem.at[c // 2], along(2)
        )

    def pass_dkv(c):
        return remote(
            relay.at[c // 2], dkv_recv.at[c], relay_send_sem.at[c // 2], dkv_recv_sem.at[c], along(-3)
        )

    def either(condition, one, other):
        @pl.when(condition)
        def _():
            one.start()

        @pl.when(jnp.logical_not(condition))
        def _():
            other.start()

    def write(c):
        return [
            pltpu.make_async_copy(out.at[n, c], dst.at[:, columns(c)], out_sem.at[c, n])
            for n, dst in enumerate((dq_hbm, dk_hbm, dv_hbm))
        ]

    stat_copies = [
        pltpu.make_async_copy(src, stats.at[0, n], stat_sem.at[n])
        for n, src in enumerate((log_hbm, delta_hbm))
    ]
    for copy in stat_copies:
        copy.start()

    @pl.loop(0, chunks)
    def _(c):
        for copy in stage(c):
            copy.start()

    barrier = pltpu.get_barrier_semaphore()
    for device in (up, down, right, left):
        pl.semaphore_signal(barrier, inc=1, device_id=device, device_id_type=MESH)
    for role, distances in partners:
        @pl.when(role)
        def _():
            for distance in distances:
                pl.semaphore_signal(barrier, inc=1, device_id=along(distance), device_id_type=MESH)
    pl.semaphore_wait(barrier, 4 + 2 * jnp.logical_or(relays, ends).astype(jnp.int32))

    for n, copy in enumerate(stat_copies):
        copy.wait()
        send_stats(n).start()

    @pl.loop(0, chunks)
    def _(c):
        for copy in stage(c):
            copy.wait()
        send_qg(c).start()
        odd = lax.rem(c, 2) == 1
        either(jnp.logical_and(sends_keys, odd), send_kv_relay(c), send_kv(c))

    for n in range(2):
        send_stats(n).wait_recv()

    @pl.when(relays_keys)
    def _():
        @pl.loop(0, chunks // 2)
        def _(pair):
            send_kv_relay(2 * pair + 1).wait_recv()
            pass_kv(2 * pair + 1).start()

    def relay_sums(c):
        send_dkv_relay(c).wait_recv()
        pass_dkv(c).start()

    first_head = lax.broadcasted_iota(jnp.int32, (1, LANES), 1) < HEAD_DIM

    @pl.loop(0, chunks)
    def _(c):
        send_qg(c).wait_recv()
        send_kv(c).wait_recv()
        queries = jnp.concatenate([qg[c, 0, 0], qg[c, 1, 0]], axis=0)
        grads = jnp.concatenate([qg[c, 0, 1], qg[c, 1, 1]], axis=0)
        keys = jnp.concatenate([kv[c, 0, 0], kv[c, 1, 0]], axis=0)
        values = jnp.concatenate([kv[c, 0, 1], kv[c, 1, 1]], axis=0)
        dq = None
        dks, dvs = [], []
        for head in range(2):
            mine = first_head if head == 0 else jnp.logical_not(first_head)
            row = 2 * c + head
            logs = jnp.concatenate([stats[0, 0, pl.ds(row, 1), :], stats[1, 0, pl.ds(row, 1), :]], axis=1)
            deltas = jnp.concatenate([stats[0, 1, pl.ds(row, 1), :], stats[1, 1, pl.ds(row, 1), :]], axis=1)
            keys_h = jnp.where(mine, keys, jnp.zeros_like(keys))
            values_h = jnp.where(mine, values, jnp.zeros_like(values))
            scores = mm(keys_h, queries, NT)
            probs = jnp.exp2(scores * (SCALE * LOG2E) - logs * LOG2E)
            dprobs = mm(values_h, grads, NT)
            score_grad = (probs * (dprobs - deltas)).astype(jnp.bfloat16)
            dvs.append(mm(probs.astype(jnp.bfloat16), grads, NN))
            dks.append(mm(score_grad, queries, NN))
            part = mm(score_grad, keys_h, TN)
            dq = part if dq is None else dq + part
        dk = jnp.where(first_head, dks[0], dks[1]) * SCALE
        dv = jnp.where(first_head, dvs[0], dvs[1])
        dq = dq * SCALE
        rows = dq.shape[0] // 2
        dq_send[c] = dq[rows:].astype(jnp.bfloat16)
        send_dq(c).start()
        dkv_send[c, 0] = dk[rows:].astype(jnp.bfloat16)
        dkv_send[c, 1] = dv[rows:].astype(jnp.bfloat16)
        odd = lax.rem(c, 2) == 1
        either(jnp.logical_and(sends_sums, odd), send_dkv_relay(c), send_dkv(c))

        @pl.when(jnp.logical_and(relays_sums, jnp.logical_and(odd, c > 2)))
        def _():
            relay_sums(c - 2)

        dq_own[c] = dq[:rows]
        dkv_own[c, 0] = dk[:rows]
        dkv_own[c, 1] = dv[:rows]

    @pl.when(relays_sums)
    def _():
        relay_sums(chunks - 1)

    @pl.loop(0, chunks)
    def _(c):
        send_dq(c).wait_recv()
        out[0, c] = (dq_own[c] + dq_recv[c].astype(jnp.float32)).astype(jnp.bfloat16)
        send_dkv(c).wait_recv()
        for n in range(2):
            total = dkv_own[c, n] + dkv_recv[c, n].astype(jnp.float32)
            out[1 + n, c] = total.astype(jnp.bfloat16)
        for copy in write(c):
            copy.start()

    for n in range(2):
        send_stats(n).wait_send()

    @pl.when(relays)
    def _():
        @pl.loop(0, chunks // 2)
        def _(pair):
            pass_kv(2 * pair + 1).wait_send()

    @pl.loop(0, chunks)
    def _(c):
        send_qg(c).wait_send()
        send_kv(c).wait_send()
        send_dq(c).wait_send()
        send_dkv(c).wait_send()
        for copy in write(c):
            copy.wait()


def body(queries, key_states, value_states, out_grad, log_total, row_delta):
    rows, width = queries.shape
    heads = log_total.shape[0]
    chunks = width // LANES
    dma = pltpu.SemaphoreType.DMA
    low, full = jnp.bfloat16, jnp.float32
    block = jax.ShapeDtypeStruct((rows, width), low)
    return pl.pallas_call(
        functools.partial(
            kernel, lax.axis_size("outer"), lax.axis_size("inner"), chunks
        ),
        out_shape=(block, block, block),
        in_specs=[pl.BlockSpec(memory_space=pl.ANY)] * 6,
        out_specs=[pl.BlockSpec(memory_space=pl.ANY)] * 3,
        scratch_shapes=[
            pltpu.VMEM((chunks, 2, 2, rows, LANES), low),
            pltpu.VMEM((chunks, 2, 2, rows, LANES), low),
            pltpu.VMEM((chunks // 2, 2, rows, LANES), low),
            pltpu.VMEM((2, 2, heads, rows), full),
            pltpu.VMEM((chunks, rows, LANES), full),
            pltpu.VMEM((chunks, 2, rows, LANES), full),
            pltpu.VMEM((chunks, rows, LANES), low),
            pltpu.VMEM((chunks, 2, rows, LANES), low),
            pltpu.VMEM((chunks, rows, LANES), low),
            pltpu.VMEM((chunks, 2, rows, LANES), low),
            pltpu.VMEM((3, chunks, rows, LANES), low),
            dma((chunks, 4)), dma((2,)),
            dma((chunks,)), dma((chunks,)), dma((chunks,)), dma((chunks,)),
            dma((2,)), dma((2,)),
            dma((chunks,)), dma((chunks,)), dma((chunks,)), dma((chunks,)),
            dma((chunks, 3)),
            dma((chunks // 2,)), dma((chunks // 2,)),
        ],
        compiler_params=pltpu.CompilerParams(
            collective_id=0, has_side_effects=True, vmem_limit_bytes=60 * 2**20
        ),
        cost_estimate=pl.CostEstimate(
            flops=40 * rows * rows * width, bytes_accessed=14 * rows * width,
            transcendentals=4 * heads * rows * rows,
        ),
        name="window_backward",
    )(queries, key_states, value_states, out_grad, log_total, row_delta)


def solution(mesh):
    tokens = P(("outer", "inner"), None)
    stats = P(None, ("outer", "inner"))
    return jax.shard_map(
        body,
        mesh=mesh,
        in_specs=(tokens, tokens, tokens, tokens, stats, stats),
        out_specs=(tokens, tokens, tokens),
        check_vma=False,
    )
```

```python
import functools
import math

import jax
import jax.numpy as jnp
from jax import lax
from jax.experimental import pallas as pl
from jax.experimental.pallas import tpu as pltpu
from jax.sharding import PartitionSpec as P

HEAD_DIM = 64
SCALE = HEAD_DIM ** (-0.5)
LOG2E = math.log2(math.e)
LANES = 128
RUN = 8
DIRECT = 5
LAG = 6
ROUTES = (1, 2, 3)
MESH = pl.DeviceIdType.MESH
NT = (((1,), (1,)), ((), ()))
NN = (((1,), (0,)), ((), ()))
TN = (((0,), (0,)), ((), ()))


def mm(a, b, dims):
    return lax.dot_general(a, b, dims, preferred_element_type=jnp.float32)


def kernel(
    n_outer, n_inner, chunks,
    q_hbm, k_hbm, v_hbm, g_hbm, log_hbm, delta_hbm,
    dq_hbm, dk_hbm, dv_hbm,
    qg, kv, relay, stats, dq_own, dkv_own, dq_send, dkv_send, dq_recv, dkv_recv, out,
    stage_sem, stat_sem, qg_send_sem, qg_recv_sem, kv_send_sem, kv_recv_sem,
    st_send_sem, st_recv_sem, dq_send_sem, dq_recv_sem, dkv_send_sem, dkv_recv_sem, out_sem,
    relay_send_sem, relay_recv_sem,
):
    o, i = lax.axis_index("outer"), lax.axis_index("inner")
    up = (lax.rem(o + 1, n_outer), i)
    down = (lax.rem(o + n_outer - 1, n_outer), i)
    right = (o, lax.rem(i + 1, n_inner))
    left = (o, lax.rem(i + n_inner - 1, n_inner))

    place = lax.rem(i, RUN)
    sends_keys, sends_sums = place == RUN - 1, place == 0
    ends = jnp.logical_or(sends_keys, sends_sums)
    relays = jnp.logical_not(ends)
    relays_keys = jnp.logical_and(relays, lax.rem(place, 2) == 1)
    relays_sums = jnp.logical_and(relays, lax.rem(place, 2) == 0)
    odd_place = lax.rem(place, 2) == 1
    route = (place + 1) // 2
    units = (2 * chunks - DIRECT) // 3

    def along(distance):
        return (o, lax.rem(i + (distance + n_inner), n_inner))

    def key_relay(k):
        return along(2 * k - RUN)

    def sum_relay(k):
        return along(2 * k)

    key_source, key_target = along(RUN - 2 * route), along(RUN + 1 - 2 * route)
    sum_source, sum_target = along(-2 * route), along(-2 * route - 1)
    partners = (
        (sends_keys, [key_relay(k) for k in ROUTES] + [along(2 * k + 1) for k in ROUTES]),
        (sends_sums, [sum_relay(k) for k in ROUTES] + [along(2 * k - RUN - 1) for k in ROUTES]),
        (relays_keys, [key_source, key_target]),
        (relays_sums, [sum_source, sum_target]),
    )

    def columns(c):
        return pl.ds(pl.multiple_of(c * LANES, LANES), LANES)

    def stage(c):
        sources = ((q_hbm, qg, 0), (g_hbm, qg, 1), (k_hbm, kv, 0), (v_hbm, kv, 1))
        return [
            pltpu.make_async_copy(src.at[:, columns(c)], dst.at[c, 0, at], stage_sem.at[c, n])
            for n, (src, dst, at) in enumerate(sources)
        ]

    def remote(src, dst, send, recv, device):
        return pltpu.make_async_remote_copy(
            src_ref=src, dst_ref=dst, send_sem=send, recv_sem=recv,
            device_id=device, device_id_type=MESH,
        )

    def send_qg(c):
        return remote(qg.at[c, 0], qg.at[c, 1], qg_send_sem.at[c], qg_recv_sem.at[c], down)

    def send_kv(c):
        return remote(kv.at[c, 0], kv.at[c, 1], kv_send_sem.at[c], kv_recv_sem.at[c], right)

    def send_kv_routes(c):
        for n in range(2):
            u = 2 * c + n

            @pl.when(u < DIRECT)
            def _():
                remote(
                    kv.at[c, 0, n], kv.at[c, 1, n], kv_send_sem.at[c], kv_recv_sem.at[c], right
                ).start()

            @pl.when(u >= DIRECT)
            def _():
                k, j = 1 + lax.rem(u - DIRECT + 3, 3), jnp.maximum(u - DIRECT, 0) // 3
                remote(
                    kv.at[c, 0, n], relay.at[j], kv_send_sem.at[c], relay_recv_sem.at[j], key_relay(k)
                ).start()

    def pass_kv(j):
        u = DIRECT + 3 * j + route - 1
        c, n = u // 2, lax.rem(u, 2)
        return remote(relay.at[j], kv.at[c, 1, n], relay_send_sem.at[j], kv_recv_sem.at[c], key_target)

    def arrived(j):
        return remote(relay.at[j], relay.at[j], relay_send_sem.at[j], relay_recv_sem.at[j], right)

    def send_stats(n):
        return remote(stats.at[0, n], stats.at[1, n], st_send_sem.at[n], st_recv_sem.at[n], down)

    def send_dq(c):
        return remote(dq_send.at[c], dq_recv.at[c], dq_send_sem.at[c], dq_recv_sem.at[c], up)

    def send_dkv(c):
        return remote(dkv_send.at[c], dkv_recv.at[c], dkv_send_sem.at[c], dkv_recv_sem.at[c], left)

    def send_dkv_routes(c):
        for n in range(2):
            u = 2 * c + n

            @pl.when(u >= 2 * chunks - DIRECT)
            def _():
                remote(
                    dkv_send.at[c, n], dkv_recv.at[c, n], dkv_send_sem.at[c], dkv_recv_sem.at[c], left
                ).start()

            @pl.when(u < 2 * chunks - DIRECT)
            def _():
                k, j = 1 + lax.rem(u, 3), jnp.minimum(u // 3, units - 1)
                remote(
                    dkv_send.at[c, n], relay.at[j], dkv_send_sem.at[c], relay_recv_sem.at[j], sum_relay(k)
                ).start()

    def pass_dkv(j):
        u = 3 * j + route - 1
        c, n = u // 2, lax.rem(u, 2)
        return remote(relay.at[j], dkv_recv.at[c, n], relay_send_sem.at[j], dkv_recv_sem.at[c], sum_target)

    def spread(condition, c, one, by_route):
        @pl.when(condition)
        def _():
            by_route(c)

        @pl.when(jnp.logical_not(condition))
        def _():
            one.start()

    def write(c):
        return [
            pltpu.make_async_copy(out.at[n, c], dst.at[:, columns(c)], out_sem.at[c, n])
            for n, dst in enumerate((dq_hbm, dk_hbm, dv_hbm))
        ]

    stat_copies = [
        pltpu.make_async_copy(src, stats.at[0, n], stat_sem.at[n])
        for n, src in enumerate((log_hbm, delta_hbm))
    ]
    for copy in stat_copies:
        copy.start()

    @pl.loop(0, chunks)
    def _(c):
        for copy in stage(c):
            copy.start()

    barrier = pltpu.get_barrier_semaphore()
    for device in (up, down, right, left):
        pl.semaphore_signal(barrier, inc=1, device_id=device, device_id_type=MESH)
    for role, devices in partners:
        @pl.when(role)
        def _():
            for device in devices:
                pl.semaphore_signal(barrier, inc=1, device_id=device, device_id_type=MESH)
    pl.semaphore_wait(barrier, 6 + 4 * ends.astype(jnp.int32))

    for n, copy in enumerate(stat_copies):
        copy.wait()
        send_stats(n).start()

    @pl.loop(0, chunks)
    def _(c):
        for copy in stage(c):
            copy.wait()
        spread(sends_keys, c, send_kv(c), send_kv_routes)

        @pl.when(jnp.logical_not(odd_place))
        def _():
            send_qg(c).start()

    @pl.when(relays_keys)
    def _():
        @pl.loop(0, units)
        def _(j):
            arrived(j).wait_recv()
            pass_kv(j).start()

    @pl.when(odd_place)
    def _():
        @pl.loop(0, chunks)
        def _(c):
            send_qg(c).start()

    def pass_sums(j):
        arrived(j).wait_recv()
        pass_dkv(j).start()

    for n in range(2):
        send_stats(n).wait_recv()

    first_head = lax.broadcasted_iota(jnp.int32, (1, LANES), 1) < HEAD_DIM

    @pl.loop(0, chunks)
    def _(c):
        @pl.when(jnp.logical_and(relays_sums, jnp.logical_and(lax.rem(c, 2) == 0, c >= LAG)))
        def _():
            pass_sums((c - LAG) // 2)

        send_qg(c).wait_recv()
        send_kv(c).wait_recv()
        queries = jnp.concatenate([qg[c, 0, 0], qg[c, 1, 0]], axis=0)
        grads = jnp.concatenate([qg[c, 0, 1], qg[c, 1, 1]], axis=0)
        keys = jnp.concatenate([kv[c, 0, 0], kv[c, 1, 0]], axis=0)
        values = jnp.concatenate([kv[c, 0, 1], kv[c, 1, 1]], axis=0)
        dq = None
        dks, dvs = [], []
        for head in range(2):
            mine = first_head if head == 0 else jnp.logical_not(first_head)
            row = 2 * c + head
            logs = jnp.concatenate([stats[0, 0, pl.ds(row, 1), :], stats[1, 0, pl.ds(row, 1), :]], axis=1)
            deltas = jnp.concatenate([stats[0, 1, pl.ds(row, 1), :], stats[1, 1, pl.ds(row, 1), :]], axis=1)
            keys_h = jnp.where(mine, keys, jnp.zeros_like(keys))
            values_h = jnp.where(mine, values, jnp.zeros_like(values))
            scores = mm(keys_h, queries, NT)
            probs = jnp.exp2(scores * (SCALE * LOG2E) - logs * LOG2E)
            dprobs = mm(values_h, grads, NT)
            score_grad = (probs * (dprobs - deltas)).astype(jnp.bfloat16)
            dvs.append(mm(probs.astype(jnp.bfloat16), grads, NN))
            dks.append(mm(score_grad, queries, NN))
            part = mm(score_grad, keys_h, TN)
            dq = part if dq is None else dq + part
        dk = jnp.where(first_head, dks[0], dks[1]) * SCALE
        dv = jnp.where(first_head, dvs[0], dvs[1])
        dq = dq * SCALE
        rows = dq.shape[0] // 2
        dq_send[c] = dq[rows:].astype(jnp.bfloat16)
        send_dq(c).start()
        dkv_send[c, 0] = dk[rows:].astype(jnp.bfloat16)
        dkv_send[c, 1] = dv[rows:].astype(jnp.bfloat16)
        spread(sends_sums, c, send_dkv(c), send_dkv_routes)
        dq_own[c] = dq[:rows]
        dkv_own[c, 0] = dk[:rows]
        dkv_own[c, 1] = dv[:rows]

    @pl.when(relays_sums)
    def _():
        @pl.loop((chunks - LAG) // 2, units)
        def _(j):
            pass_sums(j)

    @pl.loop(0, chunks)
    def _(c):
        send_dq(c).wait_recv()
        out[0, c] = (dq_own[c] + dq_recv[c].astype(jnp.float32)).astype(jnp.bfloat16)
        send_dkv(c).wait_recv()
        for n in range(2):
            total = dkv_own[c, n] + dkv_recv[c, n].astype(jnp.float32)
            out[1 + n, c] = total.astype(jnp.bfloat16)
        for copy in write(c):
            copy.start()

    for n in range(2):
        send_stats(n).wait_send()

    @pl.when(relays)
    def _():
        @pl.loop(0, units)
        def _(j):
            arrived(j).wait_send()

    @pl.loop(0, chunks)
    def _(c):
        send_qg(c).wait_send()
        send_kv(c).wait_send()
        send_dq(c).wait_send()
        send_dkv(c).wait_send()
        for copy in write(c):
            copy.wait()


def body(queries, key_states, value_states, out_grad, log_total, row_delta):
    rows, width = queries.shape
    heads = log_total.shape[0]
    chunks = width // LANES
    dma = pltpu.SemaphoreType.DMA
    low, full = jnp.bfloat16, jnp.float32
    block = jax.ShapeDtypeStruct((rows, width), low)
    return pl.pallas_call(
        functools.partial(
            kernel, lax.axis_size("outer"), lax.axis_size("inner"), chunks
        ),
        out_shape=(block, block, block),
        in_specs=[pl.BlockSpec(memory_space=pl.ANY)] * 6,
        out_specs=[pl.BlockSpec(memory_space=pl.ANY)] * 3,
        scratch_shapes=[
            pltpu.VMEM((chunks, 2, 2, rows, LANES), low),
            pltpu.VMEM((chunks, 2, 2, rows, LANES), low),
            pltpu.VMEM((chunks // 2, rows, LANES), low),
            pltpu.VMEM((2, 2, heads, rows), full),
            pltpu.VMEM((chunks, rows, LANES), full),
            pltpu.VMEM((chunks, 2, rows, LANES), full),
            pltpu.VMEM((chunks, rows, LANES), low),
            pltpu.VMEM((chunks, 2, rows, LANES), low),
            pltpu.VMEM((chunks, rows, LANES), low),
            pltpu.VMEM((chunks, 2, rows, LANES), low),
            pltpu.VMEM((3, chunks, rows, LANES), low),
            dma((chunks, 4)), dma((2,)),
            dma((chunks,)), dma((chunks,)), dma((chunks,)), dma((chunks,)),
            dma((2,)), dma((2,)),
            dma((chunks,)), dma((chunks,)), dma((chunks,)), dma((chunks,)),
            dma((chunks, 3)),
            dma((chunks // 2,)), dma((chunks // 2,)),
        ],
        compiler_params=pltpu.CompilerParams(
            collective_id=0, has_side_effects=True, vmem_limit_bytes=60 * 2**20
        ),
        cost_estimate=pl.CostEstimate(
            flops=40 * rows * rows * width, bytes_accessed=14 * rows * width,
            transcendentals=4 * heads * rows * rows,
        ),
        name="window_backward",
    )(queries, key_states, value_states, out_grad, log_total, row_delta)


def solution(mesh):
    tokens = P(("outer", "inner"), None)
    stats = P(None, ("outer", "inner"))
    return jax.shard_map(
        body,
        mesh=mesh,
        in_specs=(tokens, tokens, tokens, tokens, stats, stats),
        out_specs=(tokens, tokens, tokens),
        check_vma=False,
    )
```

```python
import functools
import math

import jax
import jax.numpy as jnp
from jax import lax
from jax.experimental import pallas as pl
from jax.experimental.pallas import tpu as pltpu
from jax.sharding import PartitionSpec as P

HEAD_DIM = 64
SCALE = HEAD_DIM ** (-0.5)
LOG2E = math.log2(math.e)
LANES = 128
RUN = 8
DIRECT = 5
LAG = 6
ROUTES = (1, 2, 3)
MESH = pl.DeviceIdType.MESH
NT = (((1,), (1,)), ((), ()))
NN = (((1,), (0,)), ((), ()))


def mm(a, b, dims):
    return lax.dot_general(a, b, dims, preferred_element_type=jnp.float32)


def kernel(
    n_outer, n_inner, chunks,
    q_hbm, k_hbm, v_hbm, g_hbm, log_hbm, delta_hbm,
    dq_hbm, dk_hbm, dv_hbm,
    qg, kv, relay, stats, dq_own, dkv_own, dq_send, dkv_send, dq_recv, dkv_recv, out,
    stage_sem, stat_sem, qg_send_sem, qg_recv_sem, kv_send_sem, kv_recv_sem,
    st_send_sem, st_recv_sem, dq_send_sem, dq_recv_sem, dkv_send_sem, dkv_recv_sem, out_sem,
    relay_send_sem, relay_recv_sem,
):
    o, i = lax.axis_index("outer"), lax.axis_index("inner")
    up = (lax.rem(o + 1, n_outer), i)
    down = (lax.rem(o + n_outer - 1, n_outer), i)
    right = (o, lax.rem(i + 1, n_inner))
    left = (o, lax.rem(i + n_inner - 1, n_inner))

    place = lax.rem(i, RUN)
    sends_keys, sends_sums = place == RUN - 1, place == 0
    ends = jnp.logical_or(sends_keys, sends_sums)
    relays = jnp.logical_not(ends)
    relays_keys = jnp.logical_and(relays, lax.rem(place, 2) == 1)
    relays_sums = jnp.logical_and(relays, lax.rem(place, 2) == 0)
    odd_place = lax.rem(place, 2) == 1
    rows = q_hbm.shape[0]
    holds_dq = jnp.logical_and(lax.rem(o, 4) == 2, jnp.logical_not(odd_place))
    route = (place + 1) // 2
    units = (2 * chunks - DIRECT) // 3

    def along(distance):
        return (o, lax.rem(i + (distance + n_inner), n_inner))

    def key_relay(k):
        return along(2 * k - RUN)

    def sum_relay(k):
        return along(2 * k)

    key_source, key_target = along(RUN - 2 * route), along(RUN + 1 - 2 * route)
    sum_source, sum_target = along(-2 * route), along(-2 * route - 1)
    partners = (
        (sends_keys, [key_relay(k) for k in ROUTES] + [along(2 * k + 1) for k in ROUTES]),
        (sends_sums, [sum_relay(k) for k in ROUTES] + [along(2 * k - RUN - 1) for k in ROUTES]),
        (relays_keys, [key_source, key_target]),
        (relays_sums, [sum_source, sum_target]),
    )

    def columns(c):
        return pl.ds(pl.multiple_of(c * LANES, LANES), LANES)

    def stage(c):
        sources = ((q_hbm, qg, 0), (g_hbm, qg, 1), (k_hbm, kv, 0), (v_hbm, kv, 1))
        return [
            pltpu.make_async_copy(src.at[:, columns(c)], dst.at[c, 0, at], stage_sem.at[c, n])
            for n, (src, dst, at) in enumerate(sources)
        ]

    def remote(src, dst, send, recv, device):
        return pltpu.make_async_remote_copy(
            src_ref=src, dst_ref=dst, send_sem=send, recv_sem=recv,
            device_id=device, device_id_type=MESH,
        )

    def send_qg(c):
        return remote(qg.at[c, 0], qg.at[c, 1], qg_send_sem.at[c], qg_recv_sem.at[c], down)

    def send_kv(c):
        return remote(kv.at[c, 0], kv.at[c, 1], kv_send_sem.at[c], kv_recv_sem.at[c], right)

    def send_kv_routes(c):
        for n in range(2):
            u = 2 * c + n

            @pl.when(u < DIRECT)
            def _():
                remote(
                    kv.at[c, 0, n], kv.at[c, 1, n], kv_send_sem.at[c], kv_recv_sem.at[c], right
                ).start()

            @pl.when(u >= DIRECT)
            def _():
                k, j = 1 + lax.rem(u - DIRECT + 3, 3), jnp.maximum(u - DIRECT, 0) // 3
                remote(
                    kv.at[c, 0, n], relay.at[j], kv_send_sem.at[c], relay_recv_sem.at[j], key_relay(k)
                ).start()

    def pass_kv(j):
        u = DIRECT + 3 * j + route - 1
        c, n = u // 2, lax.rem(u, 2)
        return remote(relay.at[j], kv.at[c, 1, n], relay_send_sem.at[j], kv_recv_sem.at[c], key_target)

    def arrived(j):
        return remote(relay.at[j], relay.at[j], relay_send_sem.at[j], relay_recv_sem.at[j], right)

    def send_stats(n):
        return remote(stats.at[0, n], stats.at[1, n], st_send_sem.at[n], st_recv_sem.at[n], down)

    def send_dq(c):
        return remote(dq_send.at[c], dq_recv.at[c], dq_send_sem.at[c], dq_recv_sem.at[c], up)

    def send_dkv(c):
        return remote(dkv_send.at[c], dkv_recv.at[c], dkv_send_sem.at[c], dkv_recv_sem.at[c], left)

    def send_dkv_routes(c):
        for n in range(2):
            u = 2 * c + n

            @pl.when(u >= 2 * chunks - DIRECT)
            def _():
                remote(
                    dkv_send.at[c, n], dkv_recv.at[c, n], dkv_send_sem.at[c], dkv_recv_sem.at[c], left
                ).start()

            @pl.when(u < 2 * chunks - DIRECT)
            def _():
                k, j = 1 + lax.rem(u, 3), jnp.minimum(u // 3, units - 1)
                remote(
                    dkv_send.at[c, n], relay.at[j], dkv_send_sem.at[c], relay_recv_sem.at[j], sum_relay(k)
                ).start()

    def pass_dkv(j):
        u = 3 * j + route - 1
        c, n = u // 2, lax.rem(u, 2)
        return remote(relay.at[j], dkv_recv.at[c, n], relay_send_sem.at[j], dkv_recv_sem.at[c], sum_target)

    def spread(condition, c, one, by_route):
        @pl.when(condition)
        def _():
            by_route(c)

        @pl.when(jnp.logical_not(condition))
        def _():
            one.start()

    def write(c):
        return [
            pltpu.make_async_copy(out.at[n, c], dst.at[:, columns(c)], out_sem.at[c, n])
            for n, dst in enumerate((dq_hbm, dk_hbm, dv_hbm))
        ]

    stat_copies = [
        pltpu.make_async_copy(src, stats.at[0, n], stat_sem.at[n])
        for n, src in enumerate((log_hbm, delta_hbm))
    ]
    for copy in stat_copies:
        copy.start()

    @pl.loop(0, chunks)
    def _(c):
        for copy in stage(c):
            copy.start()

    barrier = pltpu.get_barrier_semaphore()
    for device in (up, down, right, left):
        pl.semaphore_signal(barrier, inc=1, device_id=device, device_id_type=MESH)
    for role, devices in partners:
        @pl.when(role)
        def _():
            for device in devices:
                pl.semaphore_signal(barrier, inc=1, device_id=device, device_id_type=MESH)
    pl.semaphore_wait(barrier, 6 + 4 * ends.astype(jnp.int32))

    for n, copy in enumerate(stat_copies):
        copy.wait()
        send_stats(n).start()

    @pl.loop(0, chunks)
    def _(c):
        for copy in stage(c):
            copy.wait()
        spread(sends_keys, c, send_kv(c), send_kv_routes)

        @pl.when(jnp.logical_not(odd_place))
        def _():
            send_qg(c).start()

    @pl.when(relays_keys)
    def _():
        @pl.loop(0, units)
        def _(j):
            arrived(j).wait_recv()
            pass_kv(j).start()

    @pl.when(odd_place)
    def _():
        @pl.loop(0, chunks)
        def _(c):
            send_qg(c).start()

    def pass_sums(j):
        arrived(j).wait_recv()
        pass_dkv(j).start()

    for n in range(2):
        send_stats(n).wait_recv()

    lanes = lax.broadcasted_iota(jnp.int32, (1, LANES), 1)
    heads_of = (lanes < HEAD_DIM, lanes >= HEAD_DIM)

    def stat(n, row):
        return jnp.concatenate([stats[0, n, pl.ds(row, 1), :], stats[1, n, pl.ds(row, 1), :]], axis=1)

    def terms(c, keys, values):
        queries = jnp.concatenate([qg[c, 0, 0], qg[c, 1, 0]], axis=0)
        grads = jnp.concatenate([qg[c, 0, 1], qg[c, 1, 1]], axis=0)
        scores = [mm(jnp.where(mine, keys, jnp.zeros_like(keys)), queries, NT) for mine in heads_of]
        dprobs = [mm(jnp.where(mine, values, jnp.zeros_like(values)), grads, NT) for mine in heads_of]
        probs = [
            jnp.exp2(scores[h] * (SCALE * LOG2E) - stat(0, 2 * c + h) * LOG2E) for h in range(2)
        ]
        score_grad = [
            (probs[h] * (dprobs[h] - stat(1, 2 * c + h))).astype(jnp.bfloat16) for h in range(2)
        ]
        dv = [mm(part.astype(jnp.bfloat16), grads, NN) for part in probs]
        dk = [mm(part, queries, NN) for part in score_grad]
        keys_t = jnp.transpose(keys)
        dq = [
            mm(keys_t[h * HEAD_DIM:(h + 1) * HEAD_DIM], score_grad[h], NN) for h in range(2)
        ]
        return (
            jnp.transpose(jnp.concatenate(dq, axis=0)) * SCALE,
            jnp.where(heads_of[0], dk[0], dk[1]) * SCALE,
            jnp.where(heads_of[0], dv[0], dv[1]),
        )

    def send_back(c, dq, dk_left, dv_left):
        dq_send[c] = dq[rows:].astype(jnp.bfloat16)

        @pl.when(jnp.logical_not(holds_dq))
        def _():
            send_dq(c).start()

        dkv_send[c, 0] = dk_left.astype(jnp.bfloat16)
        dkv_send[c, 1] = dv_left.astype(jnp.bfloat16)
        spread(sends_sums, c, send_dkv(c), send_dkv_routes)
        dq_own[c] = dq[:rows]

    def keep(c, dk, dv):
        dkv_own[c, 0] = dk
        dkv_own[c, 1] = dv

    @pl.loop(0, chunks)
    def _(c):
        @pl.when(jnp.logical_and(relays_sums, jnp.logical_and(lax.rem(c, 2) == 0, c >= LAG)))
        def _():
            pass_sums((c - LAG) // 2)

        send_qg(c).wait_recv()
        send_kv(c).wait_recv()

        keys = jnp.concatenate([kv[c, 0, 0], kv[c, 1, 0]], axis=0)
        values = jnp.concatenate([kv[c, 0, 1], kv[c, 1, 1]], axis=0)
        dq, dk, dv = terms(c, keys, values)
        send_back(c, dq, dk[rows:], dv[rows:])
        keep(c, dk[:rows], dv[:rows])

    @pl.when(relays_sums)
    def _():
        @pl.loop((chunks - LAG) // 2, units)
        def _(j):
            pass_sums(j)

    @pl.when(holds_dq)
    def _():
        @pl.loop(0, chunks)
        def _(c):
            send_dq(c).start()

    @pl.loop(0, chunks)
    def _(c):
        send_dq(c).wait_recv()
        out[0, c] = (dq_own[c] + dq_recv[c].astype(jnp.float32)).astype(jnp.bfloat16)
        send_dkv(c).wait_recv()
        for n in range(2):
            total = dkv_own[c, n] + dkv_recv[c, n].astype(jnp.float32)
            out[1 + n, c] = total.astype(jnp.bfloat16)
        for copy in write(c):
            copy.start()

    for n in range(2):
        send_stats(n).wait_send()

    @pl.when(relays)
    def _():
        @pl.loop(0, units)
        def _(j):
            arrived(j).wait_send()

    @pl.loop(0, chunks)
    def _(c):
        send_qg(c).wait_send()
        send_kv(c).wait_send()
        send_dq(c).wait_send()
        send_dkv(c).wait_send()
        for copy in write(c):
            copy.wait()


def body(queries, key_states, value_states, out_grad, log_total, row_delta):
    rows, width = queries.shape
    heads = log_total.shape[0]
    chunks = width // LANES
    dma = pltpu.SemaphoreType.DMA
    low, full = jnp.bfloat16, jnp.float32
    block = jax.ShapeDtypeStruct((rows, width), low)
    return pl.pallas_call(
        functools.partial(
            kernel, lax.axis_size("outer"), lax.axis_size("inner"), chunks
        ),
        out_shape=(block, block, block),
        in_specs=[pl.BlockSpec(memory_space=pl.ANY)] * 6,
        out_specs=[pl.BlockSpec(memory_space=pl.ANY)] * 3,
        scratch_shapes=[
            pltpu.VMEM((chunks, 2, 2, rows, LANES), low),
            pltpu.VMEM((chunks, 2, 2, rows, LANES), low),
            pltpu.VMEM((chunks // 2, rows, LANES), low),
            pltpu.VMEM((2, 2, heads, rows), full),
            pltpu.VMEM((chunks, rows, LANES), full),
            pltpu.VMEM((chunks, 2, rows, LANES), full),
            pltpu.VMEM((chunks, rows, LANES), low),
            pltpu.VMEM((chunks, 2, rows, LANES), low),
            pltpu.VMEM((chunks, rows, LANES), low),
            pltpu.VMEM((chunks, 2, rows, LANES), low),
            pltpu.VMEM((3, chunks, rows, LANES), low),
            dma((chunks, 4)), dma((2,)),
            dma((chunks,)), dma((chunks,)), dma((chunks,)), dma((chunks,)),
            dma((2,)), dma((2,)),
            dma((chunks,)), dma((chunks,)), dma((chunks,)), dma((chunks,)),
            dma((chunks, 3)),
            dma((chunks // 2,)), dma((chunks // 2,)),
        ],
        compiler_params=pltpu.CompilerParams(
            collective_id=0, has_side_effects=True, vmem_limit_bytes=60 * 2**20
        ),
        cost_estimate=pl.CostEstimate(
            flops=40 * rows * rows * width, bytes_accessed=14 * rows * width,
            transcendentals=4 * heads * rows * rows,
        ),
        name="window_backward",
    )(queries, key_states, value_states, out_grad, log_total, row_delta)


def solution(mesh):
    tokens = P(("outer", "inner"), None)
    stats = P(None, ("outer", "inner"))
    return jax.shard_map(
        body,
        mesh=mesh,
        in_specs=(tokens, tokens, tokens, tokens, stats, stats),
        out_specs=(tokens, tokens, tokens),
        check_vma=False,
    )
```

```python
import functools
import math

import jax
import jax.numpy as jnp
from jax import lax
from jax.experimental import pallas as pl
from jax.experimental.pallas import tpu as pltpu
from jax.sharding import PartitionSpec as P

HEAD_DIM = 64
SCALE = HEAD_DIM ** (-0.5)
LOG2E = math.log2(math.e)
LANES = 128
RUN = 8
DIRECT = 5
LAG = 6
AHEAD = 4
ROUTES = (1, 2, 3)
MESH = pl.DeviceIdType.MESH
NT = (((1,), (1,)), ((), ()))
NN = (((1,), (0,)), ((), ()))


def mm(a, b, dims):
    return lax.dot_general(a, b, dims, preferred_element_type=jnp.float32)


def kernel(
    n_outer, n_inner, chunks,
    q_hbm, k_hbm, v_hbm, g_hbm, log_hbm, delta_hbm,
    dq_hbm, dk_hbm, dv_hbm,
    qg, kv, relay, stats, dq_own, dkv_own, dq_send, dkv_send, dq_recv, dkv_recv, out,
    stage_sem, stat_sem, qg_send_sem, qg_recv_sem, kv_send_sem, kv_recv_sem,
    st_send_sem, st_recv_sem, dq_send_sem, dq_recv_sem, dkv_send_sem, dkv_recv_sem, out_sem,
    relay_send_sem, relay_recv_sem, row_sem,
):
    o, i = lax.axis_index("outer"), lax.axis_index("inner")
    up = (lax.rem(o + 1, n_outer), i)
    down = (lax.rem(o + n_outer - 1, n_outer), i)
    right = (o, lax.rem(i + 1, n_inner))
    left = (o, lax.rem(i + n_inner - 1, n_inner))

    place = lax.rem(i, RUN)
    sends_keys, sends_sums = place == RUN - 1, place == 0
    ends = jnp.logical_or(sends_keys, sends_sums)
    relays = jnp.logical_not(ends)
    relays_keys = jnp.logical_and(relays, lax.rem(place, 2) == 1)
    relays_sums = jnp.logical_and(relays, lax.rem(place, 2) == 0)
    odd_place = lax.rem(place, 2) == 1
    rows = q_hbm.shape[0]
    holds_dq = jnp.logical_and(lax.rem(o, 4) == 2, jnp.logical_not(odd_place))
    route = (place + 1) // 2
    units = (2 * chunks - DIRECT) // 3

    first_row, last_row = o == 0, o == n_outer - 1
    ahead = jnp.where(last_row, AHEAD, chunks)

    def along(distance):
        return (o, lax.rem(i + (distance + n_inner), n_inner))

    def key_relay(k):
        return along(2 * k - RUN)

    def sum_relay(k):
        return along(2 * k)

    key_source, key_target = along(RUN - 2 * route), along(RUN + 1 - 2 * route)
    sum_source, sum_target = along(-2 * route), along(-2 * route - 1)
    partners = (
        (sends_keys, [key_relay(k) for k in ROUTES] + [along(2 * k + 1) for k in ROUTES]),
        (sends_sums, [sum_relay(k) for k in ROUTES] + [along(2 * k - RUN - 1) for k in ROUTES]),
        (relays_keys, [key_source, key_target]),
        (relays_sums, [sum_source, sum_target]),
    )

    def columns(c):
        return pl.ds(pl.multiple_of(c * LANES, LANES), LANES)

    def stage(c):
        sources = ((q_hbm, qg, 0), (g_hbm, qg, 1), (k_hbm, kv, 0), (v_hbm, kv, 1))
        return [
            pltpu.make_async_copy(src.at[:, columns(c)], dst.at[c, 0, at], stage_sem.at[c, n])
            for n, (src, dst, at) in enumerate(sources)
        ]

    def remote(src, dst, send, recv, device):
        return pltpu.make_async_remote_copy(
            src_ref=src, dst_ref=dst, send_sem=send, recv_sem=recv,
            device_id=device, device_id_type=MESH,
        )

    def send_qg(c):
        return remote(qg.at[c, 0], qg.at[c, 1], qg_send_sem.at[c], qg_recv_sem.at[c], down)

    def send_kv(c):
        return remote(kv.at[c, 0], kv.at[c, 1], kv_send_sem.at[c], kv_recv_sem.at[c], right)

    def send_kv_routes(c):
        for n in range(2):
            u = 2 * c + n

            @pl.when(u < DIRECT)
            def _():
                remote(
                    kv.at[c, 0, n], kv.at[c, 1, n], kv_send_sem.at[c], kv_recv_sem.at[c], right
                ).start()

            @pl.when(u >= DIRECT)
            def _():
                k, j = 1 + lax.rem(u - DIRECT + 3, 3), jnp.maximum(u - DIRECT, 0) // 3
                remote(
                    kv.at[c, 0, n], relay.at[j], kv_send_sem.at[c], relay_recv_sem.at[j], key_relay(k)
                ).start()

    def pass_kv(j):
        u = DIRECT + 3 * j + route - 1
        c, n = u // 2, lax.rem(u, 2)
        return remote(relay.at[j], kv.at[c, 1, n], relay_send_sem.at[j], kv_recv_sem.at[c], key_target)

    def arrived(j):
        return remote(relay.at[j], relay.at[j], relay_send_sem.at[j], relay_recv_sem.at[j], right)

    def send_stats(n):
        return remote(stats.at[0, n], stats.at[1, n], st_send_sem.at[n], st_recv_sem.at[n], down)

    def send_dq(c):
        return remote(dq_send.at[c], dq_recv.at[c], dq_send_sem.at[c], dq_recv_sem.at[c], up)

    def send_dkv(c):
        return remote(dkv_send.at[c], dkv_recv.at[c], dkv_send_sem.at[c], dkv_recv_sem.at[c], left)

    def send_dkv_routes(c):
        for n in range(2):
            u = 2 * c + n

            @pl.when(u >= 2 * chunks - DIRECT)
            def _():
                remote(
                    dkv_send.at[c, n], dkv_recv.at[c, n], dkv_send_sem.at[c], dkv_recv_sem.at[c], left
                ).start()

            @pl.when(u < 2 * chunks - DIRECT)
            def _():
                k, j = 1 + lax.rem(u, 3), jnp.minimum(u // 3, units - 1)
                remote(
                    dkv_send.at[c, n], relay.at[j], dkv_send_sem.at[c], relay_recv_sem.at[j], sum_relay(k)
                ).start()

    def pass_dkv(j):
        u = 3 * j + route - 1
        c, n = u // 2, lax.rem(u, 2)
        return remote(relay.at[j], dkv_recv.at[c, n], relay_send_sem.at[j], dkv_recv_sem.at[c], sum_target)

    def spread(condition, c, one, by_route):
        @pl.when(condition)
        def _():
            by_route(c)

        @pl.when(jnp.logical_not(condition))
        def _():
            one.start()

    def write(c):
        return [
            pltpu.make_async_copy(out.at[n, c], dst.at[:, columns(c)], out_sem.at[c, n])
            for n, dst in enumerate((dq_hbm, dk_hbm, dv_hbm))
        ]

    stat_copies = [
        pltpu.make_async_copy(src, stats.at[0, n], stat_sem.at[n])
        for n, src in enumerate((log_hbm, delta_hbm))
    ]
    for copy in stat_copies:
        copy.start()

    @pl.loop(0, chunks)
    def _(c):
        for copy in stage(c):
            copy.start()

    barrier = pltpu.get_barrier_semaphore()
    for device in (down, right, left):
        pl.semaphore_signal(barrier, inc=1, device_id=device, device_id_type=MESH)

    @pl.when(jnp.logical_not(last_row))
    def _():
        pl.semaphore_signal(barrier, inc=1, device_id=up, device_id_type=MESH)

    for role, devices in partners:
        @pl.when(role)
        def _():
            for device in devices:
                pl.semaphore_signal(barrier, inc=1, device_id=device, device_id_type=MESH)
    pl.semaphore_wait(barrier, 6 + 4 * ends.astype(jnp.int32) - first_row.astype(jnp.int32))

    @pl.when(last_row)
    def _():
        pl.semaphore_signal(row_sem, inc=1, device_id=up, device_id_type=MESH)

    for n, copy in enumerate(stat_copies):
        copy.wait()

        @pl.when(jnp.logical_not(first_row))
        def _():
            send_stats(n).start()


    @pl.loop(0, chunks)
    def _(c):
        for copy in stage(c):
            copy.wait()
        spread(sends_keys, c, send_kv(c), send_kv_routes)

        @pl.when(jnp.logical_and(jnp.logical_not(jnp.logical_or(odd_place, first_row)), c < ahead))
        def _():
            send_qg(c).start()

    @pl.when(relays_keys)
    def _():
        @pl.loop(0, units)
        def _(j):
            arrived(j).wait_recv()
            pass_kv(j).start()

    @pl.when(first_row)
    def _():
        pl.semaphore_wait(row_sem, 1)
        for n in range(2):
            send_stats(n).start()

    @pl.when(jnp.logical_or(odd_place, first_row))
    def _():
        @pl.loop(0, ahead)
        def _(c):
            send_qg(c).start()

    def pass_sums(j):
        arrived(j).wait_recv()
        pass_dkv(j).start()

    for n in range(2):
        send_stats(n).wait_recv()

    lanes = lax.broadcasted_iota(jnp.int32, (1, LANES), 1)
    heads_of = (lanes < HEAD_DIM, lanes >= HEAD_DIM)

    def stat(n, row):
        return jnp.concatenate([stats[0, n, pl.ds(row, 1), :], stats[1, n, pl.ds(row, 1), :]], axis=1)

    def terms(c, keys, values):
        queries = jnp.concatenate([qg[c, 0, 0], qg[c, 1, 0]], axis=0)
        grads = jnp.concatenate([qg[c, 0, 1], qg[c, 1, 1]], axis=0)
        scores = [mm(jnp.where(mine, keys, jnp.zeros_like(keys)), queries, NT) for mine in heads_of]
        dprobs = [mm(jnp.where(mine, values, jnp.zeros_like(values)), grads, NT) for mine in heads_of]
        probs = [
            jnp.exp2(scores[h] * (SCALE * LOG2E) - stat(0, 2 * c + h) * LOG2E) for h in range(2)
        ]
        score_grad = [
            (probs[h] * (dprobs[h] - stat(1, 2 * c + h))).astype(jnp.bfloat16) for h in range(2)
        ]
        dv = [mm(part.astype(jnp.bfloat16), grads, NN) for part in probs]
        dk = [mm(part, queries, NN) for part in score_grad]
        keys_t = jnp.transpose(keys)
        dq = [
            mm(keys_t[h * HEAD_DIM:(h + 1) * HEAD_DIM], score_grad[h], NN) for h in range(2)
        ]
        return (
            jnp.transpose(jnp.concatenate(dq, axis=0)) * SCALE,
            jnp.where(heads_of[0], dk[0], dk[1]) * SCALE,
            jnp.where(heads_of[0], dv[0], dv[1]),
        )

    def send_back(c, dq, dk_left, dv_left):
        dq_send[c] = dq[rows:].astype(jnp.bfloat16)

        @pl.when(jnp.logical_not(holds_dq))
        def _():
            send_dq(c).start()

        dkv_send[c, 0] = dk_left.astype(jnp.bfloat16)
        dkv_send[c, 1] = dv_left.astype(jnp.bfloat16)
        spread(sends_sums, c, send_dkv(c), send_dkv_routes)
        dq_own[c] = dq[:rows]

    def keep(c, dk, dv):
        dkv_own[c, 0] = dk
        dkv_own[c, 1] = dv

    @pl.loop(0, chunks)
    def _(c):
        @pl.when(jnp.logical_and(relays_sums, jnp.logical_and(lax.rem(c, 2) == 0, c >= LAG)))
        def _():
            pass_sums((c - LAG) // 2)

        send_qg(c).wait_recv()
        send_kv(c).wait_recv()

        @pl.when(c + ahead < chunks)
        def _():
            send_qg(jnp.minimum(c + ahead, chunks - 1)).start()

        keys = jnp.concatenate([kv[c, 0, 0], kv[c, 1, 0]], axis=0)
        values = jnp.concatenate([kv[c, 0, 1], kv[c, 1, 1]], axis=0)
        dq, dk, dv = terms(c, keys, values)
        send_back(c, dq, dk[rows:], dv[rows:])
        keep(c, dk[:rows], dv[:rows])

    @pl.when(relays_sums)
    def _():
        @pl.loop((chunks - LAG) // 2, units)
        def _(j):
            pass_sums(j)

    @pl.when(holds_dq)
    def _():
        @pl.loop(0, chunks)
        def _(c):
            send_dq(c).start()

    @pl.loop(0, chunks)
    def _(c):
        send_dq(c).wait_recv()
        out[0, c] = (dq_own[c] + dq_recv[c].astype(jnp.float32)).astype(jnp.bfloat16)
        send_dkv(c).wait_recv()
        for n in range(2):
            total = dkv_own[c, n] + dkv_recv[c, n].astype(jnp.float32)
            out[1 + n, c] = total.astype(jnp.bfloat16)
        for copy in write(c):
            copy.start()

    for n in range(2):
        send_stats(n).wait_send()

    @pl.when(relays)
    def _():
        @pl.loop(0, units)
        def _(j):
            arrived(j).wait_send()

    @pl.loop(0, chunks)
    def _(c):
        send_qg(c).wait_send()
        send_kv(c).wait_send()
        send_dq(c).wait_send()
        send_dkv(c).wait_send()
        for copy in write(c):
            copy.wait()


def body(queries, key_states, value_states, out_grad, log_total, row_delta):
    rows, width = queries.shape
    heads = log_total.shape[0]
    chunks = width // LANES
    dma = pltpu.SemaphoreType.DMA
    low, full = jnp.bfloat16, jnp.float32
    block = jax.ShapeDtypeStruct((rows, width), low)
    return pl.pallas_call(
        functools.partial(
            kernel, lax.axis_size("outer"), lax.axis_size("inner"), chunks
        ),
        out_shape=(block, block, block),
        in_specs=[pl.BlockSpec(memory_space=pl.ANY)] * 6,
        out_specs=[pl.BlockSpec(memory_space=pl.ANY)] * 3,
        scratch_shapes=[
            pltpu.VMEM((chunks, 2, 2, rows, LANES), low),
            pltpu.VMEM((chunks, 2, 2, rows, LANES), low),
            pltpu.VMEM((chunks // 2, rows, LANES), low),
            pltpu.VMEM((2, 2, heads, rows), full),
            pltpu.VMEM((chunks, rows, LANES), full),
            pltpu.VMEM((chunks, 2, rows, LANES), full),
            pltpu.VMEM((chunks, rows, LANES), low),
            pltpu.VMEM((chunks, 2, rows, LANES), low),
            pltpu.VMEM((chunks, rows, LANES), low),
            pltpu.VMEM((chunks, 2, rows, LANES), low),
            pltpu.VMEM((3, chunks, rows, LANES), low),
            dma((chunks, 4)), dma((2,)),
            dma((chunks,)), dma((chunks,)), dma((chunks,)), dma((chunks,)),
            dma((2,)), dma((2,)),
            dma((chunks,)), dma((chunks,)), dma((chunks,)), dma((chunks,)),
            dma((chunks, 3)),
            dma((chunks // 2,)), dma((chunks // 2,)), pltpu.SemaphoreType.REGULAR,
        ],
        compiler_params=pltpu.CompilerParams(
            collective_id=0, has_side_effects=True, vmem_limit_bytes=60 * 2**20
        ),
        cost_estimate=pl.CostEstimate(
            flops=40 * rows * rows * width, bytes_accessed=14 * rows * width,
            transcendentals=4 * heads * rows * rows,
        ),
        name="window_backward",
    )(queries, key_states, value_states, out_grad, log_total, row_delta)


def solution(mesh):
    tokens = P(("outer", "inner"), None)
    stats = P(None, ("outer", "inner"))
    return jax.shard_map(
        body,
        mesh=mesh,
        in_specs=(tokens, tokens, tokens, tokens, stats, stats),
        out_specs=(tokens, tokens, tokens),
        check_vma=False,
    )
```

```python
import functools
import math

import jax
import jax.numpy as jnp
from jax import lax
from jax.experimental import pallas as pl
from jax.experimental.pallas import tpu as pltpu
from jax.sharding import PartitionSpec as P

HEAD_DIM = 64
SCALE = HEAD_DIM ** (-0.5)
LOG2E = math.log2(math.e)
LANES = 128
RUN = 8
DIRECT = 5
LAG = 6
AHEAD = 4
ROUTES = (1, 2, 3)
MESH = pl.DeviceIdType.MESH
NT = (((1,), (1,)), ((), ()))
NN = (((1,), (0,)), ((), ()))


def mm(a, b, dims):
    return lax.dot_general(a, b, dims, preferred_element_type=jnp.float32)


def kernel(
    n_outer, n_inner, chunks,
    q_hbm, k_hbm, v_hbm, g_hbm, log_hbm, delta_hbm,
    dq_out, dk_out, dv_out,
    qg, kv, relay, stats, dq_own, dkv_own, dq_send, dkv_send, dq_recv, dkv_recv,
    stage_sem, stat_sem, qg_send_sem, qg_recv_sem, kv_send_sem, kv_recv_sem,
    st_send_sem, st_recv_sem, dq_send_sem, dq_recv_sem, dkv_send_sem, dkv_recv_sem,
    relay_send_sem, relay_recv_sem, row_sem,
):
    o, i = lax.axis_index("outer"), lax.axis_index("inner")
    up = (lax.rem(o + 1, n_outer), i)
    down = (lax.rem(o + n_outer - 1, n_outer), i)
    right = (o, lax.rem(i + 1, n_inner))
    left = (o, lax.rem(i + n_inner - 1, n_inner))

    place = lax.rem(i, RUN)
    sends_keys, sends_sums = place == RUN - 1, place == 0
    ends = jnp.logical_or(sends_keys, sends_sums)
    relays = jnp.logical_not(ends)
    relays_keys = jnp.logical_and(relays, lax.rem(place, 2) == 1)
    relays_sums = jnp.logical_and(relays, lax.rem(place, 2) == 0)
    odd_place = lax.rem(place, 2) == 1
    rows = q_hbm.shape[0]
    holds_dq = jnp.logical_and(lax.rem(o, 4) == 2, jnp.logical_not(odd_place))
    route = (place + 1) // 2
    units = (2 * chunks - DIRECT) // 3

    first_row, last_row = o == 0, o == n_outer - 1
    ahead = jnp.where(last_row, AHEAD, chunks)

    def along(distance):
        return (o, lax.rem(i + (distance + n_inner), n_inner))

    def key_relay(k):
        return along(2 * k - RUN)

    def sum_relay(k):
        return along(2 * k)

    key_source, key_target = along(RUN - 2 * route), along(RUN + 1 - 2 * route)
    sum_source, sum_target = along(-2 * route), along(-2 * route - 1)
    partners = (
        (sends_keys, [key_relay(k) for k in ROUTES] + [along(2 * k + 1) for k in ROUTES]),
        (sends_sums, [sum_relay(k) for k in ROUTES] + [along(2 * k - RUN - 1) for k in ROUTES]),
        (relays_keys, [key_source, key_target]),
        (relays_sums, [sum_source, sum_target]),
    )

    def columns(c):
        return pl.ds(pl.multiple_of(c * LANES, LANES), LANES)

    def stage(c):
        sources = ((q_hbm, qg, 0), (g_hbm, qg, 1), (k_hbm, kv, 0), (v_hbm, kv, 1))
        return [
            pltpu.make_async_copy(src.at[:, columns(c)], dst.at[c, 0, at], stage_sem.at[c, n])
            for n, (src, dst, at) in enumerate(sources)
        ]

    def remote(src, dst, send, recv, device):
        return pltpu.make_async_remote_copy(
            src_ref=src, dst_ref=dst, send_sem=send, recv_sem=recv,
            device_id=device, device_id_type=MESH,
        )

    def send_qg(c):
        return remote(qg.at[c, 0], qg.at[c, 1], qg_send_sem.at[c], qg_recv_sem.at[c], down)

    def send_kv(c):
        return remote(kv.at[c, 0], kv.at[c, 1], kv_send_sem.at[c], kv_recv_sem.at[c], right)

    def send_kv_routes(c):
        for n in range(2):
            u = 2 * c + n

            @pl.when(u < DIRECT)
            def _():
                remote(
                    kv.at[c, 0, n], kv.at[c, 1, n], kv_send_sem.at[c], kv_recv_sem.at[c], right
                ).start()

            @pl.when(u >= DIRECT)
            def _():
                k, j = 1 + lax.rem(u - DIRECT + 3, 3), jnp.maximum(u - DIRECT, 0) // 3
                remote(
                    kv.at[c, 0, n], relay.at[j], kv_send_sem.at[c], relay_recv_sem.at[j], key_relay(k)
                ).start()

    def pass_kv(j):
        u = DIRECT + 3 * j + route - 1
        c, n = u // 2, lax.rem(u, 2)
        return remote(relay.at[j], kv.at[c, 1, n], relay_send_sem.at[j], kv_recv_sem.at[c], key_target)

    def arrived(j):
        return remote(relay.at[j], relay.at[j], relay_send_sem.at[j], relay_recv_sem.at[j], right)

    def send_stats(n):
        return remote(stats.at[0, n], stats.at[1, n], st_send_sem.at[n], st_recv_sem.at[n], down)

    def send_dq(c):
        return remote(dq_send.at[c], dq_recv.at[c], dq_send_sem.at[c], dq_recv_sem.at[c], up)

    def send_dkv(c):
        return remote(dkv_send.at[c], dkv_recv.at[c], dkv_send_sem.at[c], dkv_recv_sem.at[c], left)

    def send_dkv_routes(c):
        for n in range(2):
            u = 2 * c + n

            @pl.when(u >= 2 * chunks - DIRECT)
            def _():
                remote(
                    dkv_send.at[c, n], dkv_recv.at[c, n], dkv_send_sem.at[c], dkv_recv_sem.at[c], left
                ).start()

            @pl.when(u < 2 * chunks - DIRECT)
            def _():
                k, j = 1 + lax.rem(u, 3), jnp.minimum(u // 3, units - 1)
                remote(
                    dkv_send.at[c, n], relay.at[j], dkv_send_sem.at[c], relay_recv_sem.at[j], sum_relay(k)
                ).start()

    def pass_dkv(j):
        u = 3 * j + route - 1
        c, n = u // 2, lax.rem(u, 2)
        return remote(relay.at[j], dkv_recv.at[c, n], relay_send_sem.at[j], dkv_recv_sem.at[c], sum_target)

    def spread(condition, c, one, by_route):
        @pl.when(condition)
        def _():
            by_route(c)

        @pl.when(jnp.logical_not(condition))
        def _():
            one.start()

    stat_copies = [
        pltpu.make_async_copy(src, stats.at[0, n], stat_sem.at[n])
        for n, src in enumerate((log_hbm, delta_hbm))
    ]
    for copy in stat_copies:
        copy.start()

    @pl.loop(0, chunks)
    def _(c):
        for copy in stage(c):
            copy.start()

    barrier = pltpu.get_barrier_semaphore()
    for device in (down, right, left):
        pl.semaphore_signal(barrier, inc=1, device_id=device, device_id_type=MESH)

    @pl.when(jnp.logical_not(last_row))
    def _():
        pl.semaphore_signal(barrier, inc=1, device_id=up, device_id_type=MESH)

    for role, devices in partners:
        @pl.when(role)
        def _():
            for device in devices:
                pl.semaphore_signal(barrier, inc=1, device_id=device, device_id_type=MESH)
    pl.semaphore_wait(barrier, 6 + 4 * ends.astype(jnp.int32) - first_row.astype(jnp.int32))

    @pl.when(last_row)
    def _():
        pl.semaphore_signal(row_sem, inc=1, device_id=up, device_id_type=MESH)

    for n, copy in enumerate(stat_copies):
        copy.wait()

        @pl.when(jnp.logical_not(first_row))
        def _():
            send_stats(n).start()


    @pl.loop(0, chunks)
    def _(c):
        for copy in stage(c):
            copy.wait()
        spread(sends_keys, c, send_kv(c), send_kv_routes)

        @pl.when(jnp.logical_and(jnp.logical_not(jnp.logical_or(odd_place, first_row)), c < ahead))
        def _():
            send_qg(c).start()

    @pl.when(relays_keys)
    def _():
        @pl.loop(0, units)
        def _(j):
            arrived(j).wait_recv()
            pass_kv(j).start()

    @pl.when(first_row)
    def _():
        pl.semaphore_wait(row_sem, 1)
        for n in range(2):
            send_stats(n).start()

    @pl.when(jnp.logical_or(odd_place, first_row))
    def _():
        @pl.loop(0, ahead)
        def _(c):
            send_qg(c).start()

    def pass_sums(j):
        arrived(j).wait_recv()
        pass_dkv(j).start()

    for n in range(2):
        send_stats(n).wait_recv()

    lanes = lax.broadcasted_iota(jnp.int32, (1, LANES), 1)
    heads_of = (lanes < HEAD_DIM, lanes >= HEAD_DIM)

    def stat(n, row):
        return jnp.concatenate([stats[0, n, pl.ds(row, 1), :], stats[1, n, pl.ds(row, 1), :]], axis=1)

    def terms(c, keys, values):
        queries = jnp.concatenate([qg[c, 0, 0], qg[c, 1, 0]], axis=0)
        grads = jnp.concatenate([qg[c, 0, 1], qg[c, 1, 1]], axis=0)
        scores = [mm(jnp.where(mine, keys, jnp.zeros_like(keys)), queries, NT) for mine in heads_of]
        dprobs = [mm(jnp.where(mine, values, jnp.zeros_like(values)), grads, NT) for mine in heads_of]
        probs = [
            jnp.exp2(scores[h] * (SCALE * LOG2E) - stat(0, 2 * c + h) * LOG2E) for h in range(2)
        ]
        score_grad = [
            (probs[h] * (dprobs[h] - stat(1, 2 * c + h))).astype(jnp.bfloat16) for h in range(2)
        ]
        dv = [mm(part.astype(jnp.bfloat16), grads, NN) for part in probs]
        dk = [mm(part, queries, NN) for part in score_grad]
        keys_t = jnp.transpose(keys)
        dq = [
            mm(keys_t[h * HEAD_DIM:(h + 1) * HEAD_DIM], score_grad[h], NN) for h in range(2)
        ]
        return (
            jnp.transpose(jnp.concatenate(dq, axis=0)) * SCALE,
            jnp.where(heads_of[0], dk[0], dk[1]) * SCALE,
            jnp.where(heads_of[0], dv[0], dv[1]),
        )

    def send_back(c, dq, dk_left, dv_left):
        dq_send[c] = dq[rows:].astype(jnp.bfloat16)

        @pl.when(jnp.logical_not(holds_dq))
        def _():
            send_dq(c).start()

        dkv_send[c, 0] = dk_left.astype(jnp.bfloat16)
        dkv_send[c, 1] = dv_left.astype(jnp.bfloat16)
        spread(sends_sums, c, send_dkv(c), send_dkv_routes)
        dq_own[c] = dq[:rows]

    def keep(c, dk, dv):
        dkv_own[c, 0] = dk
        dkv_own[c, 1] = dv

    @pl.loop(0, chunks)
    def _(c):
        @pl.when(jnp.logical_and(relays_sums, jnp.logical_and(lax.rem(c, 2) == 0, c >= LAG)))
        def _():
            pass_sums((c - LAG) // 2)

        send_qg(c).wait_recv()
        send_kv(c).wait_recv()

        @pl.when(c + ahead < chunks)
        def _():
            send_qg(jnp.minimum(c + ahead, chunks - 1)).start()

        keys = jnp.concatenate([kv[c, 0, 0], kv[c, 1, 0]], axis=0)
        values = jnp.concatenate([kv[c, 0, 1], kv[c, 1, 1]], axis=0)
        dq, dk, dv = terms(c, keys, values)
        send_back(c, dq, dk[rows:], dv[rows:])
        keep(c, dk[:rows], dv[:rows])

    @pl.when(relays_sums)
    def _():
        @pl.loop((chunks - LAG) // 2, units)
        def _(j):
            pass_sums(j)

    @pl.when(holds_dq)
    def _():
        @pl.loop(0, chunks)
        def _(c):
            send_dq(c).start()

    @pl.loop(0, chunks)
    def _(c):
        send_dq(c).wait_recv()
        dq_out[:, columns(c)] = (dq_own[c] + dq_recv[c].astype(jnp.float32)).astype(jnp.bfloat16)
        send_dkv(c).wait_recv()
        for n, ref in enumerate((dk_out, dv_out)):
            total = dkv_own[c, n] + dkv_recv[c, n].astype(jnp.float32)
            ref[:, columns(c)] = total.astype(jnp.bfloat16)

    for n in range(2):
        send_stats(n).wait_send()

    @pl.when(relays)
    def _():
        @pl.loop(0, units)
        def _(j):
            arrived(j).wait_send()

    @pl.loop(0, chunks)
    def _(c):
        send_qg(c).wait_send()
        send_kv(c).wait_send()
        send_dq(c).wait_send()
        send_dkv(c).wait_send()


def body(queries, key_states, value_states, out_grad, log_total, row_delta):
    rows, width = queries.shape
    heads = log_total.shape[0]
    chunks = width // LANES
    dma = pltpu.SemaphoreType.DMA
    low, full = jnp.bfloat16, jnp.float32
    block = pltpu.VMEM((rows, width), low)
    return pl.pallas_call(
        functools.partial(
            kernel, lax.axis_size("outer"), lax.axis_size("inner"), chunks
        ),
        out_shape=(block, block, block),
        in_specs=[pl.BlockSpec(memory_space=pl.ANY)] * 6,
        out_specs=[pl.BlockSpec(memory_space=pltpu.VMEM)] * 3,
        scratch_shapes=[
            pltpu.VMEM((chunks, 2, 2, rows, LANES), low),
            pltpu.VMEM((chunks, 2, 2, rows, LANES), low),
            pltpu.VMEM((chunks // 2, rows, LANES), low),
            pltpu.VMEM((2, 2, heads, rows), full),
            pltpu.VMEM((chunks, rows, LANES), full),
            pltpu.VMEM((chunks, 2, rows, LANES), full),
            pltpu.VMEM((chunks, rows, LANES), low),
            pltpu.VMEM((chunks, 2, rows, LANES), low),
            pltpu.VMEM((chunks, rows, LANES), low),
            pltpu.VMEM((chunks, 2, rows, LANES), low),
            dma((chunks, 4)), dma((2,)),
            dma((chunks,)), dma((chunks,)), dma((chunks,)), dma((chunks,)),
            dma((2,)), dma((2,)),
            dma((chunks,)), dma((chunks,)), dma((chunks,)), dma((chunks,)),
            dma((chunks // 2,)), dma((chunks // 2,)), pltpu.SemaphoreType.REGULAR,
        ],
        compiler_params=pltpu.CompilerParams(
            collective_id=0, has_side_effects=True, vmem_limit_bytes=32 * 2**20
        ),
        cost_estimate=pl.CostEstimate(
            flops=40 * rows * rows * width, bytes_accessed=14 * rows * width,
            transcendentals=4 * heads * rows * rows,
        ),
        name="window_backward",
    )(*(
        pltpu.with_memory_space_constraint(array, pltpu.HBM)
        for array in (queries, key_states, value_states, out_grad, log_total, row_delta)
    ))


def solution(mesh):
    tokens = P(("outer", "inner"), None)
    stats = P(None, ("outer", "inner"))
    return jax.shard_map(
        body,
        mesh=mesh,
        in_specs=(tokens, tokens, tokens, tokens, stats, stats),
        out_specs=(tokens, tokens, tokens),
        check_vma=False,
    )
```

```python
import functools
import math

import jax
import jax.numpy as jnp
from jax import lax
from jax.experimental import pallas as pl
from jax.experimental.pallas import tpu as pltpu
from jax.sharding import PartitionSpec as P

HEAD_DIM = 64
SCALE = HEAD_DIM ** (-0.5)
LOG2E = math.log2(math.e)
LANES = 128
RUN = 8
DIRECT = 5
LAG = 6
AHEAD = 3
ROUTES = (1, 2, 3)
MESH = pl.DeviceIdType.MESH
NT = (((1,), (1,)), ((), ()))
NN = (((1,), (0,)), ((), ()))


def mm(a, b, dims):
    return lax.dot_general(a, b, dims, preferred_element_type=jnp.float32)


def kernel(
    n_outer, n_inner, chunks,
    q_hbm, k_hbm, v_hbm, g_hbm, log_hbm, delta_hbm,
    dq_out, dk_out, dv_out,
    qg, kv, relay, stats, dq_own, dkv_own, dq_send, dkv_send, dq_recv, dkv_recv,
    stage_sem, stat_sem, qg_send_sem, qg_recv_sem, kv_send_sem, kv_recv_sem,
    st_send_sem, st_recv_sem, dq_send_sem, dq_recv_sem, dkv_send_sem, dkv_recv_sem,
    relay_send_sem, relay_recv_sem, row_sem,
):
    o, i = lax.axis_index("outer"), lax.axis_index("inner")
    up = (lax.rem(o + 1, n_outer), i)
    down = (lax.rem(o + n_outer - 1, n_outer), i)
    right = (o, lax.rem(i + 1, n_inner))
    left = (o, lax.rem(i + n_inner - 1, n_inner))

    place = lax.rem(i, RUN)
    sends_keys, sends_sums = place == RUN - 1, place == 0
    ends = jnp.logical_or(sends_keys, sends_sums)
    relays = jnp.logical_not(ends)
    relays_keys = jnp.logical_and(relays, lax.rem(place, 2) == 1)
    relays_sums = jnp.logical_and(relays, lax.rem(place, 2) == 0)
    odd_place = lax.rem(place, 2) == 1
    rows = q_hbm.shape[0]
    holds_dq = jnp.logical_and(lax.rem(o, 4) == 2, jnp.logical_not(odd_place))
    route = (place + 1) // 2
    units = (2 * chunks - DIRECT) // 3

    first_row, last_row = o == 0, o == n_outer - 1
    ahead = jnp.where(last_row, AHEAD, chunks)

    def along(distance):
        return (o, lax.rem(i + (distance + n_inner), n_inner))

    def key_relay(k):
        return along(2 * k - RUN)

    def sum_relay(k):
        return along(2 * k)

    key_source, key_target = along(RUN - 2 * route), along(RUN + 1 - 2 * route)
    sum_source, sum_target = along(-2 * route), along(-2 * route - 1)
    partners = (
        (sends_keys, [key_relay(k) for k in ROUTES] + [along(2 * k + 1) for k in ROUTES]),
        (sends_sums, [sum_relay(k) for k in ROUTES] + [along(2 * k - RUN - 1) for k in ROUTES]),
        (relays_keys, [key_source, key_target]),
        (relays_sums, [sum_source, sum_target]),
    )

    def columns(c):
        return pl.ds(pl.multiple_of(c * LANES, LANES), LANES)

    def stage(c):
        sources = ((q_hbm, qg, 0), (g_hbm, qg, 1), (k_hbm, kv, 0), (v_hbm, kv, 1))
        return [
            pltpu.make_async_copy(src.at[:, columns(c)], dst.at[c, 0, at], stage_sem.at[c, n])
            for n, (src, dst, at) in enumerate(sources)
        ]

    def remote(src, dst, send, recv, device):
        return pltpu.make_async_remote_copy(
            src_ref=src, dst_ref=dst, send_sem=send, recv_sem=recv,
            device_id=device, device_id_type=MESH,
        )

    def send_qg(c):
        return remote(qg.at[c, 0], qg.at[c, 1], qg_send_sem.at[c], qg_recv_sem.at[c], down)

    def send_kv(c):
        return remote(kv.at[c, 0], kv.at[c, 1], kv_send_sem.at[c], kv_recv_sem.at[c], right)

    def send_kv_routes(c):
        for n in range(2):
            u = 2 * c + n

            @pl.when(u < DIRECT)
            def _():
                remote(
                    kv.at[c, 0, n], kv.at[c, 1, n], kv_send_sem.at[c], kv_recv_sem.at[c], right
                ).start()

            @pl.when(u >= DIRECT)
            def _():
                k, j = 1 + lax.rem(u - DIRECT + 3, 3), jnp.maximum(u - DIRECT, 0) // 3
                remote(
                    kv.at[c, 0, n], relay.at[j], kv_send_sem.at[c], relay_recv_sem.at[j], key_relay(k)
                ).start()

    def pass_kv(j):
        u = DIRECT + 3 * j + route - 1
        c, n = u // 2, lax.rem(u, 2)
        return remote(relay.at[j], kv.at[c, 1, n], relay_send_sem.at[j], kv_recv_sem.at[c], key_target)

    def arrived(j):
        return remote(relay.at[j], relay.at[j], relay_send_sem.at[j], relay_recv_sem.at[j], right)

    def send_stats(n):
        return remote(stats.at[0, n], stats.at[1, n], st_send_sem.at[n], st_recv_sem.at[n], down)

    def send_dq(c):
        return remote(dq_send.at[c], dq_recv.at[c], dq_send_sem.at[c], dq_recv_sem.at[c], up)

    def send_dkv(c):
        return remote(dkv_send.at[c], dkv_recv.at[c], dkv_send_sem.at[c], dkv_recv_sem.at[c], left)

    def send_dkv_routes(c):
        for n in range(2):
            u = 2 * c + n

            @pl.when(u >= 2 * chunks - DIRECT)
            def _():
                remote(
                    dkv_send.at[c, n], dkv_recv.at[c, n], dkv_send_sem.at[c], dkv_recv_sem.at[c], left
                ).start()

            @pl.when(u < 2 * chunks - DIRECT)
            def _():
                k, j = 1 + lax.rem(u, 3), jnp.minimum(u // 3, units - 1)
                remote(
                    dkv_send.at[c, n], relay.at[j], dkv_send_sem.at[c], relay_recv_sem.at[j], sum_relay(k)
                ).start()

    def pass_dkv(j):
        u = 3 * j + route - 1
        c, n = u // 2, lax.rem(u, 2)
        return remote(relay.at[j], dkv_recv.at[c, n], relay_send_sem.at[j], dkv_recv_sem.at[c], sum_target)

    def spread(condition, c, one, by_route):
        @pl.when(condition)
        def _():
            by_route(c)

        @pl.when(jnp.logical_not(condition))
        def _():
            one.start()

    stat_copies = [
        pltpu.make_async_copy(src, stats.at[0, n], stat_sem.at[n])
        for n, src in enumerate((log_hbm, delta_hbm))
    ]
    for copy in stat_copies:
        copy.start()

    @pl.loop(0, chunks)
    def _(c):
        for copy in stage(c):
            copy.start()

    barrier = pltpu.get_barrier_semaphore()
    for device in (down, right, left):
        pl.semaphore_signal(barrier, inc=1, device_id=device, device_id_type=MESH)

    @pl.when(jnp.logical_not(last_row))
    def _():
        pl.semaphore_signal(barrier, inc=1, device_id=up, device_id_type=MESH)

    for role, devices in partners:
        @pl.when(role)
        def _():
            for device in devices:
                pl.semaphore_signal(barrier, inc=1, device_id=device, device_id_type=MESH)
    pl.semaphore_wait(barrier, 6 + 4 * ends.astype(jnp.int32) - first_row.astype(jnp.int32))

    @pl.when(last_row)
    def _():
        pl.semaphore_signal(row_sem, inc=1, device_id=up, device_id_type=MESH)

    for n, copy in enumerate(stat_copies):
        copy.wait()

        @pl.when(jnp.logical_not(first_row))
        def _():
            send_stats(n).start()


    @pl.loop(0, chunks)
    def _(c):
        for copy in stage(c):
            copy.wait()
        spread(sends_keys, c, send_kv(c), send_kv_routes)

        @pl.when(jnp.logical_and(jnp.logical_not(jnp.logical_or(odd_place, first_row)), c < ahead))
        def _():
            send_qg(c).start()

    @pl.when(relays_keys)
    def _():
        @pl.loop(0, units)
        def _(j):
            arrived(j).wait_recv()
            pass_kv(j).start()

    @pl.when(first_row)
    def _():
        pl.semaphore_wait(row_sem, 1)
        for n in range(2):
            send_stats(n).start()

    @pl.when(jnp.logical_or(odd_place, first_row))
    def _():
        @pl.loop(0, ahead)
        def _(c):
            send_qg(c).start()

    def pass_sums(j):
        arrived(j).wait_recv()
        pass_dkv(j).start()

    for n in range(2):
        send_stats(n).wait_recv()

    lanes = lax.broadcasted_iota(jnp.int32, (1, LANES), 1)
    heads_of = (lanes < HEAD_DIM, lanes >= HEAD_DIM)

    def stat(n, row):
        return jnp.concatenate([stats[0, n, pl.ds(row, 1), :], stats[1, n, pl.ds(row, 1), :]], axis=1)

    def terms(c, keys, values):
        queries = jnp.concatenate([qg[c, 0, 0], qg[c, 1, 0]], axis=0)
        grads = jnp.concatenate([qg[c, 0, 1], qg[c, 1, 1]], axis=0)
        scores = [mm(jnp.where(mine, keys, jnp.zeros_like(keys)), queries, NT) for mine in heads_of]
        dprobs = [mm(jnp.where(mine, values, jnp.zeros_like(values)), grads, NT) for mine in heads_of]
        probs = [
            jnp.exp2(scores[h] * (SCALE * LOG2E) - stat(0, 2 * c + h) * LOG2E) for h in range(2)
        ]
        score_grad = [
            (probs[h] * (dprobs[h] - stat(1, 2 * c + h))).astype(jnp.bfloat16) for h in range(2)
        ]
        dv = [mm(part.astype(jnp.bfloat16), grads, NN) for part in probs]
        dk = [mm(part, queries, NN) for part in score_grad]
        keys_t = jnp.transpose(keys)
        dq = [
            mm(keys_t[h * HEAD_DIM:(h + 1) * HEAD_DIM], score_grad[h], NN) for h in range(2)
        ]
        return (
            jnp.transpose(jnp.concatenate(dq, axis=0)) * SCALE,
            jnp.where(heads_of[0], dk[0], dk[1]) * SCALE,
            jnp.where(heads_of[0], dv[0], dv[1]),
        )

    def send_back(c, dq, dk_left, dv_left):
        dq_send[c] = dq[rows:].astype(jnp.bfloat16)

        @pl.when(jnp.logical_not(holds_dq))
        def _():
            send_dq(c).start()

        dkv_send[c, 0] = dk_left.astype(jnp.bfloat16)
        dkv_send[c, 1] = dv_left.astype(jnp.bfloat16)
        spread(sends_sums, c, send_dkv(c), send_dkv_routes)
        dq_own[c] = dq[:rows]

    def keep(c, dk, dv):
        dkv_own[c, 0] = dk
        dkv_own[c, 1] = dv

    @pl.loop(0, chunks)
    def _(c):
        @pl.when(jnp.logical_and(relays_sums, jnp.logical_and(lax.rem(c, 2) == 0, c >= LAG)))
        def _():
            pass_sums((c - LAG) // 2)

        send_qg(c).wait_recv()
        send_kv(c).wait_recv()

        @pl.when(c + ahead < chunks)
        def _():
            send_qg(jnp.minimum(c + ahead, chunks - 1)).start()

        keys = jnp.concatenate([kv[c, 0, 0], kv[c, 1, 0]], axis=0)
        values = jnp.concatenate([kv[c, 0, 1], kv[c, 1, 1]], axis=0)
        dq, dk, dv = terms(c, keys, values)
        send_back(c, dq, dk[rows:], dv[rows:])
        keep(c, dk[:rows], dv[:rows])

    @pl.when(relays_sums)
    def _():
        @pl.loop((chunks - LAG) // 2, units)
        def _(j):
            pass_sums(j)

    @pl.when(holds_dq)
    def _():
        @pl.loop(0, chunks)
        def _(c):
            send_dq(c).start()

    @pl.loop(0, chunks)
    def _(c):
        send_dq(c).wait_recv()
        dq_out[:, columns(c)] = (dq_own[c] + dq_recv[c].astype(jnp.float32)).astype(jnp.bfloat16)
        send_dkv(c).wait_recv()
        for n, ref in enumerate((dk_out, dv_out)):
            total = dkv_own[c, n] + dkv_recv[c, n].astype(jnp.float32)
            ref[:, columns(c)] = total.astype(jnp.bfloat16)

    for n in range(2):
        send_stats(n).wait_send()

    @pl.when(relays)
    def _():
        @pl.loop(0, units)
        def _(j):
            arrived(j).wait_send()

    @pl.loop(0, chunks)
    def _(c):
        send_qg(c).wait_send()
        send_kv(c).wait_send()
        send_dq(c).wait_send()
        send_dkv(c).wait_send()


def hand_over(dq, dk, dv, dq_out, dk_out, dv_out, sem):
    copies = [
        pltpu.make_async_copy(src, dst, sem.at[n])
        for n, (src, dst) in enumerate(((dq, dq_out), (dk, dk_out), (dv, dv_out)))
    ]
    for copy in copies:
        copy.start()
    for copy in copies:
        copy.wait()


def body(queries, key_states, value_states, out_grad, log_total, row_delta):
    rows, width = queries.shape
    heads = log_total.shape[0]
    chunks = width // LANES
    dma = pltpu.SemaphoreType.DMA
    low, full = jnp.bfloat16, jnp.float32
    block = pltpu.VMEM((rows, width), low)
    grads = pl.pallas_call(
        functools.partial(
            kernel, lax.axis_size("outer"), lax.axis_size("inner"), chunks
        ),
        out_shape=(block, block, block),
        in_specs=[pl.BlockSpec(memory_space=pl.ANY)] * 6,
        out_specs=[pl.BlockSpec(memory_space=pltpu.VMEM)] * 3,
        scratch_shapes=[
            pltpu.VMEM((chunks, 2, 2, rows, LANES), low),
            pltpu.VMEM((chunks, 2, 2, rows, LANES), low),
            pltpu.VMEM((chunks // 2, rows, LANES), low),
            pltpu.VMEM((2, 2, heads, rows), full),
            pltpu.VMEM((chunks, rows, LANES), full),
            pltpu.VMEM((chunks, 2, rows, LANES), full),
            pltpu.VMEM((chunks, rows, LANES), low),
            pltpu.VMEM((chunks, 2, rows, LANES), low),
            pltpu.VMEM((chunks, rows, LANES), low),
            pltpu.VMEM((chunks, 2, rows, LANES), low),
            dma((chunks, 4)), dma((2,)),
            dma((chunks,)), dma((chunks,)), dma((chunks,)), dma((chunks,)),
            dma((2,)), dma((2,)),
            dma((chunks,)), dma((chunks,)), dma((chunks,)), dma((chunks,)),
            dma((chunks // 2,)), dma((chunks // 2,)), pltpu.SemaphoreType.REGULAR,
        ],
        compiler_params=pltpu.CompilerParams(
            collective_id=0, has_side_effects=True, vmem_limit_bytes=32 * 2**20
        ),
        cost_estimate=pl.CostEstimate(
            flops=40 * rows * rows * width, bytes_accessed=14 * rows * width,
            transcendentals=4 * heads * rows * rows,
        ),
        name="window_backward",
    )(*(
        pltpu.with_memory_space_constraint(array, pltpu.HBM)
        for array in (queries, key_states, value_states, out_grad, log_total, row_delta)
    ))
    return pl.pallas_call(
        hand_over,
        out_shape=[pltpu.HBM((rows, width), low)] * 3,
        in_specs=[pl.BlockSpec(memory_space=pltpu.VMEM)] * 3,
        out_specs=[pl.BlockSpec(memory_space=pltpu.HBM)] * 3,
        scratch_shapes=[dma((3,))],
        name="hand_over",
    )(*(pltpu.with_memory_space_constraint(array, pltpu.VMEM) for array in grads))


def solution(mesh):
    tokens = P(("outer", "inner"), None)
    stats = P(None, ("outer", "inner"))
    return jax.shard_map(
        body,
        mesh=mesh,
        in_specs=(tokens, tokens, tokens, tokens, stats, stats),
        out_specs=(tokens, tokens, tokens),
        check_vma=False,
    )
```

```python
import functools
import math

import jax
import jax.numpy as jnp
from jax import lax
from jax.experimental import pallas as pl
from jax.experimental.pallas import tpu as pltpu
from jax.sharding import PartitionSpec as P

HEAD_DIM = 64
SCALE = HEAD_DIM ** (-0.5)
LOG2E = math.log2(math.e)
LANES = 128
RUN = 8
DIRECT = 5
LAG = 8
AHEAD = 3
ROUTES = (1, 2, 3)
MESH = pl.DeviceIdType.MESH
NT = (((1,), (1,)), ((), ()))
NN = (((1,), (0,)), ((), ()))


def mm(a, b, dims):
    return lax.dot_general(a, b, dims, preferred_element_type=jnp.float32)


def kernel(
    n_outer, n_inner, chunks,
    q_hbm, k_hbm, v_hbm, g_hbm, log_hbm, delta_hbm,
    dq_out, dk_out, dv_out,
    qg, kv, relay, stats, dq_own, dkv_own, dq_send, dkv_send, dq_recv, dkv_recv,
    stage_sem, stat_sem, qg_send_sem, qg_recv_sem, kv_send_sem, kv_recv_sem,
    st_send_sem, st_recv_sem, dq_send_sem, dq_recv_sem, dkv_send_sem, dkv_recv_sem,
    relay_send_sem, relay_recv_sem, row_sem,
):
    o, i = lax.axis_index("outer"), lax.axis_index("inner")
    up = (lax.rem(o + 1, n_outer), i)
    down = (lax.rem(o + n_outer - 1, n_outer), i)
    right = (o, lax.rem(i + 1, n_inner))
    left = (o, lax.rem(i + n_inner - 1, n_inner))

    place = lax.rem(i, RUN)
    sends_keys, sends_sums = place == RUN - 1, place == 0
    ends = jnp.logical_or(sends_keys, sends_sums)
    relays = jnp.logical_not(ends)
    relays_keys = jnp.logical_and(relays, lax.rem(place, 2) == 1)
    relays_sums = jnp.logical_and(relays, lax.rem(place, 2) == 0)
    odd_place = lax.rem(place, 2) == 1
    rows = q_hbm.shape[0]
    holds_dq = jnp.logical_and(lax.rem(o, 4) == 2, jnp.logical_not(odd_place))
    route = (place + 1) // 2
    units = (2 * chunks - DIRECT) // 3

    first_row, last_row = o == 0, o == n_outer - 1
    ahead = jnp.where(last_row, AHEAD, chunks)

    def along(distance):
        return (o, lax.rem(i + (distance + n_inner), n_inner))

    def key_relay(k):
        return along(2 * k - RUN)

    def sum_relay(k):
        return along(2 * k)

    key_source, key_target = along(RUN - 2 * route), along(RUN + 1 - 2 * route)
    sum_source, sum_target = along(-2 * route), along(-2 * route - 1)
    partners = (
        (sends_keys, [key_relay(k) for k in ROUTES] + [along(2 * k + 1) for k in ROUTES]),
        (sends_sums, [sum_relay(k) for k in ROUTES] + [along(2 * k - RUN - 1) for k in ROUTES]),
        (relays_keys, [key_source, key_target]),
        (relays_sums, [sum_source, sum_target]),
    )

    def columns(c):
        return pl.ds(pl.multiple_of(c * LANES, LANES), LANES)

    def stage(c):
        sources = ((q_hbm, qg, 0), (g_hbm, qg, 1), (k_hbm, kv, 0), (v_hbm, kv, 1))
        return [
            pltpu.make_async_copy(src.at[:, columns(c)], dst.at[c, 0, at], stage_sem.at[c, n])
            for n, (src, dst, at) in enumerate(sources)
        ]

    def remote(src, dst, send, recv, device):
        return pltpu.make_async_remote_copy(
            src_ref=src, dst_ref=dst, send_sem=send, recv_sem=recv,
            device_id=device, device_id_type=MESH,
        )

    def send_qg(c):
        return remote(qg.at[c, 0], qg.at[c, 1], qg_send_sem.at[c], qg_recv_sem.at[c], down)

    def send_kv(c):
        return remote(kv.at[c, 0], kv.at[c, 1], kv_send_sem.at[c], kv_recv_sem.at[c], right)

    def send_kv_routes(c):
        for n in range(2):
            u = 2 * c + n

            @pl.when(u < DIRECT)
            def _():
                remote(
                    kv.at[c, 0, n], kv.at[c, 1, n], kv_send_sem.at[c], kv_recv_sem.at[c], right
                ).start()

            @pl.when(u >= DIRECT)
            def _():
                k, j = 1 + lax.rem(u - DIRECT + 3, 3), jnp.maximum(u - DIRECT, 0) // 3
                remote(
                    kv.at[c, 0, n], relay.at[j], kv_send_sem.at[c], relay_recv_sem.at[j], key_relay(k)
                ).start()

    def pass_kv(j):
        u = DIRECT + 3 * j + route - 1
        c, n = u // 2, lax.rem(u, 2)
        return remote(relay.at[j], kv.at[c, 1, n], relay_send_sem.at[j], kv_recv_sem.at[c], key_target)

    def arrived(j):
        return remote(relay.at[j], relay.at[j], relay_send_sem.at[j], relay_recv_sem.at[j], right)

    def send_stats(n):
        return remote(stats.at[0, n], stats.at[1, n], st_send_sem.at[n], st_recv_sem.at[n], down)

    def send_dq(c):
        return remote(dq_send.at[c], dq_recv.at[c], dq_send_sem.at[c], dq_recv_sem.at[c], up)

    def send_dkv(c):
        return remote(dkv_send.at[c], dkv_recv.at[c], dkv_send_sem.at[c], dkv_recv_sem.at[c], left)

    def send_dkv_routes(c):
        for n in range(2):
            u = 2 * c + n

            @pl.when(u >= 2 * chunks - DIRECT)
            def _():
                remote(
                    dkv_send.at[c, n], dkv_recv.at[c, n], dkv_send_sem.at[c], dkv_recv_sem.at[c], left
                ).start()

            @pl.when(u < 2 * chunks - DIRECT)
            def _():
                k, j = 1 + lax.rem(u, 3), jnp.minimum(u // 3, units - 1)
                remote(
                    dkv_send.at[c, n], relay.at[j], dkv_send_sem.at[c], relay_recv_sem.at[j], sum_relay(k)
                ).start()

    def pass_dkv(j):
        u = 3 * j + route - 1
        c, n = u // 2, lax.rem(u, 2)
        return remote(relay.at[j], dkv_recv.at[c, n], relay_send_sem.at[j], dkv_recv_sem.at[c], sum_target)

    def spread(condition, c, one, by_route):
        @pl.when(condition)
        def _():
            by_route(c)

        @pl.when(jnp.logical_not(condition))
        def _():
            one.start()

    stat_copies = [
        pltpu.make_async_copy(src, stats.at[0, n], stat_sem.at[n])
        for n, src in enumerate((log_hbm, delta_hbm))
    ]
    for copy in stat_copies:
        copy.start()

    @pl.loop(0, chunks)
    def _(c):
        for copy in stage(c):
            copy.start()

    barrier = pltpu.get_barrier_semaphore()
    for device in (down, right, left):
        pl.semaphore_signal(barrier, inc=1, device_id=device, device_id_type=MESH)

    @pl.when(jnp.logical_not(last_row))
    def _():
        pl.semaphore_signal(barrier, inc=1, device_id=up, device_id_type=MESH)

    for role, devices in partners:
        @pl.when(role)
        def _():
            for device in devices:
                pl.semaphore_signal(barrier, inc=1, device_id=device, device_id_type=MESH)
    pl.semaphore_wait(barrier, 6 + 4 * ends.astype(jnp.int32) - first_row.astype(jnp.int32))

    @pl.when(last_row)
    def _():
        pl.semaphore_signal(row_sem, inc=1, device_id=up, device_id_type=MESH)

    for n, copy in enumerate(stat_copies):
        copy.wait()

        @pl.when(jnp.logical_not(first_row))
        def _():
            send_stats(n).start()


    @pl.loop(0, chunks)
    def _(c):
        for copy in stage(c):
            copy.wait()
        spread(sends_keys, c, send_kv(c), send_kv_routes)

        @pl.when(jnp.logical_and(jnp.logical_not(jnp.logical_or(odd_place, first_row)), c < ahead))
        def _():
            send_qg(c).start()

    @pl.when(relays_keys)
    def _():
        @pl.loop(0, units)
        def _(j):
            arrived(j).wait_recv()
            pass_kv(j).start()

    @pl.when(first_row)
    def _():
        pl.semaphore_wait(row_sem, 1)
        for n in range(2):
            send_stats(n).start()

    @pl.when(jnp.logical_or(odd_place, first_row))
    def _():
        @pl.loop(0, ahead)
        def _(c):
            send_qg(c).start()

    def pass_sums(j):
        arrived(j).wait_recv()
        pass_dkv(j).start()

    for n in range(2):
        send_stats(n).wait_recv()

    lanes = lax.broadcasted_iota(jnp.int32, (1, LANES), 1)
    heads_of = (lanes < HEAD_DIM, lanes >= HEAD_DIM)

    def stat(n, row):
        return jnp.concatenate([stats[0, n, pl.ds(row, 1), :], stats[1, n, pl.ds(row, 1), :]], axis=1)

    def terms(c, keys, values):
        queries = jnp.concatenate([qg[c, 0, 0], qg[c, 1, 0]], axis=0)
        grads = jnp.concatenate([qg[c, 0, 1], qg[c, 1, 1]], axis=0)
        scores = [mm(jnp.where(mine, keys, jnp.zeros_like(keys)), queries, NT) for mine in heads_of]
        dprobs = [mm(jnp.where(mine, values, jnp.zeros_like(values)), grads, NT) for mine in heads_of]
        probs = [
            jnp.exp2(scores[h] * (SCALE * LOG2E) - stat(0, 2 * c + h) * LOG2E) for h in range(2)
        ]
        score_grad = [
            (probs[h] * (dprobs[h] - stat(1, 2 * c + h))).astype(jnp.bfloat16) for h in range(2)
        ]
        dv = [mm(part.astype(jnp.bfloat16), grads, NN) for part in probs]
        dk = [mm(part, queries, NN) for part in score_grad]
        keys_t = jnp.transpose(keys)
        dq = [
            mm(keys_t[h * HEAD_DIM:(h + 1) * HEAD_DIM], score_grad[h], NN) for h in range(2)
        ]
        return (
            jnp.transpose(jnp.concatenate(dq, axis=0)) * SCALE,
            jnp.where(heads_of[0], dk[0], dk[1]) * SCALE,
            jnp.where(heads_of[0], dv[0], dv[1]),
        )

    def send_back(c, dq, dk_left, dv_left):
        dq_send[c] = dq[rows:].astype(jnp.bfloat16)

        @pl.when(jnp.logical_not(holds_dq))
        def _():
            send_dq(c).start()

        dkv_send[c, 0] = dk_left.astype(jnp.bfloat16)
        dkv_send[c, 1] = dv_left.astype(jnp.bfloat16)
        spread(sends_sums, c, send_dkv(c), send_dkv_routes)
        dq_own[c] = dq[:rows]

    def keep(c, dk, dv):
        dkv_own[c, 0] = dk
        dkv_own[c, 1] = dv

    @pl.loop(0, chunks)
    def _(c):
        @pl.when(jnp.logical_and(relays_sums, jnp.logical_and(lax.rem(c, 2) == 0, c >= LAG)))
        def _():
            pass_sums((c - LAG) // 2)

        send_qg(c).wait_recv()
        send_kv(c).wait_recv()

        @pl.when(c + ahead < chunks)
        def _():
            send_qg(jnp.minimum(c + ahead, chunks - 1)).start()

        keys = jnp.concatenate([kv[c, 0, 0], kv[c, 1, 0]], axis=0)
        values = jnp.concatenate([kv[c, 0, 1], kv[c, 1, 1]], axis=0)
        dq, dk, dv = terms(c, keys, values)
        send_back(c, dq, dk[rows:], dv[rows:])
        keep(c, dk[:rows], dv[:rows])

    @pl.when(relays_sums)
    def _():
        @pl.loop((chunks - LAG) // 2, units)
        def _(j):
            pass_sums(j)

    @pl.when(holds_dq)
    def _():
        @pl.loop(0, chunks)
        def _(c):
            send_dq(c).start()

    @pl.loop(0, chunks)
    def _(c):
        send_dq(c).wait_recv()
        dq_out[:, columns(c)] = (dq_own[c] + dq_recv[c].astype(jnp.float32)).astype(jnp.bfloat16)
        send_dkv(c).wait_recv()
        for n, ref in enumerate((dk_out, dv_out)):
            total = dkv_own[c, n] + dkv_recv[c, n].astype(jnp.float32)
            ref[:, columns(c)] = total.astype(jnp.bfloat16)

    for n in range(2):
        send_stats(n).wait_send()

    @pl.when(relays)
    def _():
        @pl.loop(0, units)
        def _(j):
            arrived(j).wait_send()

    @pl.loop(0, chunks)
    def _(c):
        send_qg(c).wait_send()
        send_kv(c).wait_send()
        send_dq(c).wait_send()
        send_dkv(c).wait_send()


def hand_over(dq, dk, dv, dq_out, dk_out, dv_out, sem):
    copies = [
        pltpu.make_async_copy(src, dst, sem.at[n])
        for n, (src, dst) in enumerate(((dq, dq_out), (dk, dk_out), (dv, dv_out)))
    ]
    for copy in copies:
        copy.start()
    for copy in copies:
        copy.wait()


def body(queries, key_states, value_states, out_grad, log_total, row_delta):
    rows, width = queries.shape
    heads = log_total.shape[0]
    chunks = width // LANES
    dma = pltpu.SemaphoreType.DMA
    low, full = jnp.bfloat16, jnp.float32
    block = pltpu.VMEM((rows, width), low)
    grads = pl.pallas_call(
        functools.partial(
            kernel, lax.axis_size("outer"), lax.axis_size("inner"), chunks
        ),
        out_shape=(block, block, block),
        in_specs=[pl.BlockSpec(memory_space=pl.ANY)] * 6,
        out_specs=[pl.BlockSpec(memory_space=pltpu.VMEM)] * 3,
        scratch_shapes=[
            pltpu.VMEM((chunks, 2, 2, rows, LANES), low),
            pltpu.VMEM((chunks, 2, 2, rows, LANES), low),
            pltpu.VMEM((chunks // 2, rows, LANES), low),
            pltpu.VMEM((2, 2, heads, rows), full),
            pltpu.VMEM((chunks, rows, LANES), full),
            pltpu.VMEM((chunks, 2, rows, LANES), full),
            pltpu.VMEM((chunks, rows, LANES), low),
            pltpu.VMEM((chunks, 2, rows, LANES), low),
            pltpu.VMEM((chunks, rows, LANES), low),
            pltpu.VMEM((chunks, 2, rows, LANES), low),
            dma((chunks, 4)), dma((2,)),
            dma((chunks,)), dma((chunks,)), dma((chunks,)), dma((chunks,)),
            dma((2,)), dma((2,)),
            dma((chunks,)), dma((chunks,)), dma((chunks,)), dma((chunks,)),
            dma((chunks // 2,)), dma((chunks // 2,)), pltpu.SemaphoreType.REGULAR,
        ],
        compiler_params=pltpu.CompilerParams(
            collective_id=0, has_side_effects=True, vmem_limit_bytes=32 * 2**20
        ),
        cost_estimate=pl.CostEstimate(
            flops=40 * rows * rows * width, bytes_accessed=14 * rows * width,
            transcendentals=4 * heads * rows * rows,
        ),
        name="window_backward",
    )(*(
        pltpu.with_memory_space_constraint(array, pltpu.HBM)
        for array in (queries, key_states, value_states, out_grad, log_total, row_delta)
    ))
    return pl.pallas_call(
        hand_over,
        out_shape=[pltpu.HBM((rows, width), low)] * 3,
        in_specs=[pl.BlockSpec(memory_space=pltpu.VMEM)] * 3,
        out_specs=[pl.BlockSpec(memory_space=pltpu.HBM)] * 3,
        scratch_shapes=[dma((3,))],
        name="hand_over",
    )(*(pltpu.with_memory_space_constraint(array, pltpu.VMEM) for array in grads))


def solution(mesh):
    tokens = P(("outer", "inner"), None)
    stats = P(None, ("outer", "inner"))
    return jax.shard_map(
        body,
        mesh=mesh,
        in_specs=(tokens, tokens, tokens, tokens, stats, stats),
        out_specs=(tokens, tokens, tokens),
        check_vma=False,
    )
```
